128 devices in a mesh: row: 8 (over y_lo, x), col: 16 (over z, y_hi, core).
Axes of the slice: x: 4, y: 4 (y_hi: 2, y_lo: 2; y = y_hi * 2 + y_lo), z: 4, core: 2. Of those that a mesh axis runs over, the one named last changes fastest.
Arguments:
- voltages: float32 [1, 2, 2, 16777216], P(None, None, None, ('row', 'col')), may hold values from -6 to 6
- chirp_phase: float32 [1, 128, 131072], P(None, ('row', 'col')), may hold values from -3.140625 to 3.140625
Outputs:
- dedispersed: float32 [1, 2, 2, 16777216], P(None, None, None, ('row', 'col'))
The draws below stay inside these ranges and needn't reach their ends.
All inputs are finite; a program needn't handle non-finite values.
Results may differ from the reference program's by a relative error of at most 0.00014.
Values sent between devices are 32-bit elements; how exact they have to be, the bound alone decides.
A program may use at most 128 MiB of HBM per device.

```python
import jax
import jax.numpy as jnp

CHANNELS = 1
POLS = 2
SEG = 131072
PIECES = 128
FFT_LEN = 16777216


def block_levels(stream_key, shape, pieces, low, top_value):
    level = 1.0
    for position, blocks in pieces:
        steps = jax.random.uniform(jax.random.fold_in(jax.random.fold_in(stream_key, 6), position), (blocks,), jnp.float32, low / len(pieces), top_value / len(pieces))
        level = level * jnp.repeat(jnp.exp(steps), shape[position] // blocks).reshape((-1,) + (1,) * (len(shape) - 1 - position))
    return level


def gaussian(key, dims, spread, reach, split=(), dtype=jnp.bfloat16):
    factor_of = block_levels(key, dims, split, -0.22, 0.18) if split else 1.0
    values = jax.random.normal(key, dims, jnp.float32) * spread * factor_of
    return jnp.minimum(jnp.maximum(values, -reach), reach).astype(dtype)


def setup_inputs(seed: int = 0) -> dict:
    seeds = jax.random.split(jax.random.key(seed), 3)
    return {
        "voltages": gaussian(seeds[0], (CHANNELS, POLS, 2, FFT_LEN), 1.0, 6.0, ((3, 128),), jnp.float32),
        "chirp_phase": jnp.clip(jax.random.uniform(seeds[1], (CHANNELS, PIECES, SEG), jnp.float32, -3.140625, 3.140625), -3.140625, 3.140625),
    }


def reference(voltages, chirp_phase):
    signal = voltages[:, :, 0, :] + 1j * voltages[:, :, 1, :]
    spectrum = jnp.fft.fft(signal, axis=-1)
    angles = jnp.swapaxes(chirp_phase, 1, 2).reshape(CHANNELS, FFT_LEN)
    response = jnp.cos(angles) + 1j * jnp.sin(angles)
    filtered = spectrum * response[:, None, :]
    restored = jnp.fft.ifft(filtered, axis=-1)
    return jnp.stack([jnp.real(restored), jnp.imag(restored)], axis=2)
```

```python
import itertools
import math

import jax
import jax.numpy as jnp
import ml_dtypes
import numpy as np
from jax import lax
from jax.experimental import pallas as pl
from jax.experimental.pallas import tpu as pltpu
from jax.sharding import PartitionSpec as P

MESH = pl.DeviceIdType.MESH
F32 = jnp.float32
BF16 = jnp.bfloat16
PIECES = 128
LANES = 128
BLOCKS = 8
SEG = PIECES * BLOCKS * LANES
TOTAL = PIECES * SEG
DEVICE_DIMS = (2, 4, 4, 2, 2)
TILE = (8, 128)
SIZES = {"x": 4, "y": 4, "z": 4, "c": 2}
ORDERS = (("xc", "yz"), ("yz", "xc"), ("xc", "yz"), ("yz", "xc"))
STREAMS = 4
EXCHANGES = 4


def unit_roots(index, modulus):
    angles = -2.0 * math.pi * (index % modulus) / modulus
    return np.cos(angles), np.sin(angles)


def three_pass(matrix, axis):
    high = matrix.astype(ml_dtypes.bfloat16)
    low = (matrix - high.astype(np.float64)).astype(ml_dtypes.bfloat16)
    return np.concatenate([high, high, low], axis)


def tables():
    idx = np.arange(128, dtype=np.int64)
    re, im = unit_roots(idx[:, None] * idx[None, :], 128)
    left = lambda r, i: np.block([[r, -i], [i, r]])
    right = lambda r, i: np.block([[r, i], [-i, r]])
    offsets = np.arange(BLOCKS * LANES, dtype=np.int64).reshape(BLOCKS, 1, LANES)
    grid = offsets * idx[None, :, None]
    kb = np.arange(BLOCKS, dtype=np.int64)
    small = kb[:, None] * idx[None, :]
    f32 = lambda pair, axis: np.stack(pair, axis).astype(np.float32)
    return {
        "roots": f32((re, im), 0),
        "shift": f32(unit_roots(idx[:, None] * idx[None, :], 16384), 0),
        "outer": f32(unit_roots(grid, TOTAL), 1),
        "inner": f32(unit_roots(grid, SEG), 1),
        "small": f32(unit_roots(small, BLOCKS * LANES), 1),
        "left_fwd": three_pass(left(re, im), 1),
        "left_inv": three_pass(left(re, -im) / SEG, 1),
        "right_fwd": three_pass(right(re, im), 0),
        "right_inv": three_pass(right(re, -im), 0),
    }


TABLES = tables()
NAMES = tuple(TABLES)


def split(value):
    high = value.astype(BF16)
    low = (value - high.astype(F32)).astype(BF16)
    return high, low


def left_product(matrix, real, imag):
    high, low = split(jnp.concatenate([real, imag], 0))
    out = jnp.dot(matrix, jnp.concatenate([high, low, high], 0), preferred_element_type=F32)
    return out[:128], out[128:]


def right_product(value, matrix):
    high, low = split(value)
    return jnp.dot(jnp.concatenate([high, low, high], 1), matrix, preferred_element_type=F32)


def times(real, imag, cos, sin):
    return real * cos - imag * sin, real * sin + imag * cos


def times_conj(real, imag, cos, sin):
    return real * cos + imag * sin, imag * cos - real * sin


def add(a, b):
    return a[0] + b[0], a[1] + b[1]


def sub(a, b):
    return a[0] - b[0], a[1] - b[1]


def quarter(a, sign):
    return (-a[1], a[0]) if sign > 0 else (a[1], -a[0])


def dft4(z, sign):
    e0, e1 = add(z[0], z[2]), sub(z[0], z[2])
    o0, o1 = add(z[1], z[3]), quarter(sub(z[1], z[3]), sign)
    return [add(e0, o0), add(e1, o1), sub(e0, o0), sub(e1, o1)]


def dft8(z, sign):
    even, odd = dft4(z[0::2], sign), dft4(z[1::2], sign)
    root = math.sqrt(0.5)
    q1 = quarter(odd[1], sign)
    q3 = quarter(odd[3], sign)
    odd = [
        odd[0],
        ((odd[1][0] + q1[0]) * root, (odd[1][1] + q1[1]) * root),
        quarter(odd[2], sign),
        ((q3[0] - odd[3][0]) * root, (q3[1] - odd[3][1]) * root),
    ]
    return [add(even[k], odd[k]) for k in range(4)] + [sub(even[k], odd[k]) for k in range(4)]


def sin_cos(angle):
    half = angle * 0.5
    sq = half * half
    sine = 0.0
    for power in (13, 11, 9, 7, 5, 3, 1):
        sine = sine * sq + (-1.0) ** (power // 2) / math.factorial(power)
    cosine = 0.0
    for power in (12, 10, 8, 6, 4, 2, 0):
        cosine = cosine * sq + (-1.0) ** (power // 2) / math.factorial(power)
    sine = sine * half
    return 2.0 * sine * cosine, 1.0 - 2.0 * sine * sine


def where_is(coord):
    every = slice(None)
    y = coord.get("y")
    return (
        every if y is None else y % 2,
        coord.get("x", every),
        coord.get("z", every),
        every if y is None else y // 2,
        coord.get("c", every),
    )


def device_at(coord):
    y = coord["y"]
    return ((y % 2) * 4 + coord["x"], coord["z"] * 4 + (y // 2) * 2 + coord["c"])


def slot(exchange, stage):
    return exchange * 3 + stage - 1


SLOTS = 3 * EXCHANGES - 2


def kernel(x_ref, chirp_ref, *refs):
    count = len(NAMES)
    table_refs, out_ref, refs = refs[:count], refs[count], refs[count + 1 :]
    held, refs = dict(zip(NAMES, refs[:count])), refs[count:]
    (bufs, chirp_in, response, work, lanes_work, dev_fwd, dev_inv, send_sem, recv_sem, load_sem) = refs

    row, col = lax.axis_index("row"), lax.axis_index("col")
    me = row * 16 + col
    here = {"x": row % 4, "y": row // 4 + 2 * (col // 2 % 2), "z": col // 4, "c": col % 2}

    loads = {}
    for i, (name, src) in enumerate(zip(NAMES + ("chirp",), table_refs + (chirp_ref,))):
        dst = chirp_in if name == "chirp" else held[name]
        loads[name] = pltpu.make_async_copy(src, dst, load_sem.at[i])

    def peers(axes):
        for steps in itertools.product(*[range(SIZES[a]) for a in axes]):
            there = dict(here)
            for axis, step in zip(axes, steps):
                there[axis] = (here[axis] + step) % SIZES[axis]
            yield any(steps), there

    barrier = pltpu.get_barrier_semaphore()
    greeted = [there for axes in ORDERS[0] for remote, there in peers(axes) if remote]
    for there in greeted:
        pl.semaphore_signal(barrier, inc=1, device_id=device_at(there), device_id_type=MESH)
    for name in ("roots", "shift", "chirp", "outer", "left_fwd", "inner", "small", "right_fwd", "right_inv", "left_inv"):
        loads[name].start()
    pl.semaphore_wait(barrier, len(greeted))

    def stage_ref(stream, exchange, stage):
        if exchange == 0 and stage == 0:
            return x_ref.at[stream // 2, stream % 2]
        if exchange == EXCHANGES - 1 and stage == 2:
            return out_ref.at[stream // 2, stream % 2]
        return bufs.at[stream, slot(exchange, stage)]

    def sub_ref(stream, exchange, stage, where):
        if exchange == 0 and stage == 0:
            return x_ref.at[(stream // 2,) + where + (stream % 2,)]
        if exchange == EXCHANGES - 1 and stage == 2:
            return out_ref.at[(stream // 2,) + where + (stream % 2,)]
        return bufs.at[(stream, slot(exchange, stage)) + where]

    def sem_index(exchange, phase):
        return exchange * 2 + phase

    def send(stream, exchange, phase):
        axes = ORDERS[stream][phase]
        k = sem_index(exchange, phase)
        mine = where_is({a: here[a] for a in axes})
        for remote, there in peers(axes):
            src = sub_ref(stream, exchange, phase, where_is({a: there[a] for a in axes}))
            dst = sub_ref(stream, exchange, phase + 1, mine)
            if remote:
                pltpu.make_async_remote_copy(
                    src_ref=src,
                    dst_ref=dst,
                    send_sem=send_sem.at[stream, k],
                    recv_sem=recv_sem.at[stream, k],
                    device_id=device_at(there),
                    device_id_type=MESH,
                ).start()
            else:
                pltpu.make_async_copy(src, dst, recv_sem.at[stream, k]).start()

    def arrive(stream, exchange, phase):
        whole = sub_ref(stream, exchange, phase + 1, (slice(None),) * 5)
        pltpu.make_async_copy(whole, whole, recv_sem.at[stream, sem_index(exchange, phase)]).wait()

    def sent(stream, exchange, phase):
        share = math.prod(SIZES[a] for a in ORDERS[stream][phase])
        part = bufs.at[stream, 0].reshape(128, 8, 128).at[pl.ds(0, 128 - 128 // share)]
        pltpu.make_async_copy(part, part, send_sem.at[stream, sem_index(exchange, phase)]).wait()

    def flat(stream, exchange, stage):
        return bufs.at[stream, slot(exchange, stage)].reshape(1024, 128)

    def row_of(block, part):
        return pl.ds(block % 4 * 2 + part, 128, stride=8)

    def load_pair(refs2, block):
        out = []
        for part in range(2):
            out.append(
                jnp.concatenate([refs2[b // 4][row_of(b, part), :] for b in (block, block + 1)], 1)
            )
        return out

    def build_matrices():
        for name in ("roots", "shift"):
            loads[name].wait()
        re, im = held["roots"][0], held["roots"][1]
        sre, sim = held["shift"][0], held["shift"][1]
        on_lane = lax.broadcasted_iota(jnp.int32, (128, 128), 1) == me
        on_row = lax.broadcasted_iota(jnp.int32, (128, 128), 0) == me
        pick = lambda mask, v, axis: jnp.sum(jnp.where(mask, v, 0.0), axis=axis, keepdims=True)
        fre, fim = times(re, im, pick(on_lane, sre, 1), pick(on_lane, sim, 1))
        ire, iim = times(re, im, pick(on_row, sre, 0), pick(on_row, sim, 0))
        ire, iim = ire * (1.0 / PIECES), iim * (-1.0 / PIECES)
        for ref, r, i in ((dev_fwd, fre, fim), (dev_inv, ire, iim)):
            for half, (a, b) in enumerate(((r, -i), (i, r))):
                high, low = split(jnp.concatenate([a, b], 1))
                ref[pl.ds(half * 128, 128), :] = jnp.concatenate([high, high, low], 1)

    def build_response():
        loads["chirp"].wait()
        for kb in range(BLOCKS):
            angle = chirp_in[pl.ds(kb, 128, stride=8), :].T
            sine, cosine = sin_cos(angle)
            response[kb, 0] = cosine
            response[kb, 1] = sine

    def first_step(stream):
        src, dst = flat(stream, 0, 2), flat(stream, 1, 0)
        outer = held["outer"]
        for block in range(stream % 2 * 4, stream % 2 * 4 + 4, 2):
            real, imag = load_pair((src, src), block)
            real, imag = left_product(dev_fwd[...], real, imag)
            for i in range(2):
                b = block + i
                lanes = slice(i * 128, i * 128 + 128)
                r, m = times(real[:, lanes], imag[:, lanes], outer[b, 0], outer[b, 1])
                dst[row_of(b, 0), :] = r
                dst[row_of(b, 1), :] = m

    def middle_step(pol):
        src = [flat(2 * pol + h, 1, 2) for h in range(2)]
        dst = [flat(2 * pol + h, 2, 0) for h in range(2)]
        inner, small = held["inner"], held["small"]
        for block in range(0, BLOCKS, 2):
            real, imag = load_pair(src, block)
            real, imag = left_product(held["left_fwd"][...], real, imag)
            for i in range(2):
                b = block + i
                lanes = slice(i * 128, i * 128 + 128)
                r, m = times(real[:, lanes], imag[:, lanes], inner[b, 0], inner[b, 1])
                work[b, 0] = r
                work[b, 1] = m

        def forward(step, _):
            rows = pl.ds(pl.multiple_of(step * 8, 8), 8)
            z = dft8([(work[b, 0, rows, :], work[b, 1, rows, :]) for b in range(BLOCKS)], -1)
            for k in range(BLOCKS):
                r, m = z[k]
                if k:
                    r, m = times(r, m, small[k, 0:1, :], small[k, 1:2, :])
                lanes_work[k, rows, 0:128] = r
                lanes_work[k, rows, 128:256] = m
            return 0

        lax.fori_loop(0, 16, forward, 0)

        def across(step, _):
            ks = pl.ds(step * 2, 2)
            value = lanes_work[ks].reshape(256, 256)
            value = right_product(value, held["right_fwd"][...])
            ch = response[ks]
            cosine = ch[:, 0].reshape(256, 128)
            sine = ch[:, 1].reshape(256, 128)
            r, m = times(value[:, :128], value[:, 128:], cosine, sine)
            value = right_product(jnp.concatenate([r, m], 1), held["right_inv"][...])
            lanes_work[ks] = value.reshape(2, 128, 256)
            return 0

        lax.fori_loop(0, BLOCKS // 2, across, 0)

        def backward(step, _):
            rows = pl.ds(pl.multiple_of(step * 8, 8), 8)
            z = []
            for k in range(BLOCKS):
                r, m = lanes_work[k, rows, 0:128], lanes_work[k, rows, 128:256]
                if k:
                    r, m = times_conj(r, m, small[k, 0:1, :], small[k, 1:2, :])
                z.append((r, m))
            z = dft8(z, 1)
            for b in range(BLOCKS):
                r, m = times_conj(z[b][0], z[b][1], inner[b, 0, rows, :], inner[b, 1, rows, :])
                work[b, 0, rows, :] = r
                work[b, 1, rows, :] = m
            return 0

        lax.fori_loop(0, 16, backward, 0)

        for block in range(0, BLOCKS, 2):
            real = jnp.concatenate([work[block, 0], work[block + 1, 0]], 1)
            imag = jnp.concatenate([work[block, 1], work[block + 1, 1]], 1)
            real, imag = left_product(held["left_inv"][...], real, imag)
            for i in range(2):
                b = block + i
                lanes = slice(i * 128, i * 128 + 128)
                dst[b // 4][row_of(b, 0), :] = real[:, lanes]
                dst[b // 4][row_of(b, 1), :] = imag[:, lanes]

    def last_step(stream):
        src, dst = flat(stream, 2, 2), flat(stream, 3, 0)
        outer = held["outer"]
        for block in range(stream % 2 * 4, stream % 2 * 4 + 4, 2):
            parts = []
            for b in (block, block + 1):
                parts.append(times_conj(src[row_of(b, 0), :], src[row_of(b, 1), :], outer[b, 0], outer[b, 1]))
            real = jnp.concatenate([p[0] for p in parts], 1)
            imag = jnp.concatenate([p[1] for p in parts], 1)
            real, imag = left_product(dev_inv[...], real, imag)
            for i in range(2):
                b = block + i
                lanes = slice(i * 128, i * 128 + 128)
                dst[row_of(b, 0), :] = real[:, lanes]
                dst[row_of(b, 1), :] = imag[:, lanes]

    for stream in range(STREAMS):
        send(stream, 0, 0)
    build_matrices()
    for exchange in range(EXCHANGES):
        for pair in range(2):
            for stream in (2 * pair, 2 * pair + 1):
                arrive(stream, exchange, 0)
                send(stream, exchange, 1)
        if exchange == 0:
            build_response()
            for name in ("outer", "left_fwd", "inner", "small", "right_fwd", "right_inv", "left_inv"):
                loads[name].wait()
        for pair in range(2):
            streams = (2 * pair, 2 * pair + 1)
            if exchange == 1:
                for stream in streams:
                    arrive(stream, exchange, 1)
                middle_step(pair)
                for stream in streams:
                    send(stream, exchange + 1, 0)
                continue
            for stream in streams:
                arrive(stream, exchange, 1)
                if exchange == 0:
                    first_step(stream)
                if exchange == 2:
                    last_step(stream)
                if exchange < EXCHANGES - 1:
                    send(stream, exchange + 1, 0)
    for exchange in range(EXCHANGES):
        for phase in range(2):
            for stream in range(STREAMS):
                sent(stream, exchange, phase)


def body(voltages, chirp_phase):
    shape = (2,) + DEVICE_DIMS + (2,) + TILE
    rows = voltages.reshape(2, 2, PIECES * BLOCKS, LANES).transpose(0, 2, 1, 3).reshape(shape)
    any_space = pl.BlockSpec(memory_space=pl.ANY)
    values = [jnp.asarray(TABLES[name]) for name in NAMES]
    held = [pltpu.VMEM(v.shape, v.dtype) for v in values]
    out = pl.pallas_call(
        kernel,
        out_shape=jax.ShapeDtypeStruct(shape, F32),
        in_specs=[any_space] * (2 + len(values)),
        out_specs=any_space,
        scratch_shapes=held
        + [
            pltpu.VMEM((STREAMS, SLOTS) + DEVICE_DIMS + TILE, F32),
            pltpu.VMEM((PIECES * BLOCKS, LANES), F32),
            pltpu.VMEM((BLOCKS, 2, 128, 128), F32),
            pltpu.VMEM((BLOCKS, 2, 128, 128), F32),
            pltpu.VMEM((BLOCKS, 128, 256), F32),
            pltpu.VMEM((256, 768), BF16),
            pltpu.VMEM((256, 768), BF16),
            pltpu.SemaphoreType.DMA((STREAMS, 2 * EXCHANGES)),
            pltpu.SemaphoreType.DMA((STREAMS, 2 * EXCHANGES)),
            pltpu.SemaphoreType.DMA((len(values) + 1,)),
        ],
        name="dedisperse",
        compiler_params=pltpu.CompilerParams(
            collective_id=0, has_side_effects=True, vmem_limit_bytes=56 * 1024 * 1024
        ),
        cost_estimate=pl.CostEstimate(flops=5_000_000_000, bytes_accessed=9_000_000, transcendentals=0),
    )(rows, chirp_phase.reshape(PIECES * BLOCKS, LANES), *values)
    return out.reshape(2, PIECES * BLOCKS, 2, LANES).transpose(0, 2, 1, 3).reshape(voltages.shape)


def solution(mesh):
    placed = (P(None, None, None, ("row", "col")), P(None, ("row", "col"), None))
    return jax.shard_map(
        body,
        mesh=mesh,
        in_specs=placed,
        out_specs=P(None, None, None, ("row", "col")),
        check_vma=False,
    )
```

```python
import itertools
import math

import jax
import jax.numpy as jnp
import ml_dtypes
import numpy as np
from jax import lax
from jax.experimental import pallas as pl
from jax.experimental.pallas import tpu as pltpu
from jax.sharding import PartitionSpec as P

MESH = pl.DeviceIdType.MESH
F32 = jnp.float32
BF16 = jnp.bfloat16
PIECES = 128
LANES = 128
BLOCKS = 8
SEG = PIECES * BLOCKS * LANES
TOTAL = PIECES * SEG
DEVICE_DIMS = (2, 4, 4, 2, 2)
TILE = (8, 128)
SIZES = {"x": 4, "y": 4, "z": 4, "c": 2}
ORDERS = (("xc", "yz"), ("yz", "xc"), ("xc", "yz"), ("yz", "xc"))
STREAMS = 4
EXCHANGES = 4
UNROLL_A = 1
UNROLL_C = 1
WIDE = 2


def unit_roots(index, modulus):
    angles = -2.0 * math.pi * (index % modulus) / modulus
    return np.cos(angles), np.sin(angles)


def three_pass(matrix, axis):
    high = matrix.astype(ml_dtypes.bfloat16)
    low = (matrix - high.astype(np.float64)).astype(ml_dtypes.bfloat16)
    return np.concatenate([high, high, low], axis)


def tables():
    idx = np.arange(128, dtype=np.int64)
    re, im = unit_roots(idx[:, None] * idx[None, :], 128)
    left = lambda r, i: np.block([[r, -i], [i, r]])
    right = lambda r, i: np.block([[r, i], [-i, r]])
    offsets = np.arange(BLOCKS * LANES, dtype=np.int64).reshape(BLOCKS, 1, LANES)
    grid = offsets * idx[None, :, None]
    kb = np.arange(BLOCKS, dtype=np.int64)
    small = kb[:, None] * idx[None, :]
    f32 = lambda pair, axis: np.stack(pair, axis).astype(np.float32)
    return {
        "roots": f32((re, im), 0),
        "shift": f32(unit_roots(idx[:, None] * idx[None, :], 16384), 0),
        "outer": f32(unit_roots(grid, TOTAL), 1),
        "inner": f32(unit_roots(grid, SEG), 1),
        "small": f32(unit_roots(small, BLOCKS * LANES), 1),
        "left_fwd": three_pass(left(re, im), 1),
        "left_inv": three_pass(left(re, -im) / SEG, 1),
        "right_fwd": three_pass(right(re, im), 0),
        "right_inv": three_pass(right(re, -im), 0),
    }


TABLES = tables()
NAMES = tuple(TABLES)


def split(value):
    high = value.astype(BF16)
    low = (value - high.astype(F32)).astype(BF16)
    return high, low


def left_product(matrix, real, imag):
    high, low = split(jnp.concatenate([real, imag], 0))
    out = jnp.dot(matrix, jnp.concatenate([high, low, high], 0), preferred_element_type=F32)
    return out[:128], out[128:]


def right_product(value, matrix):
    high, low = split(value)
    return jnp.dot(jnp.concatenate([high, low, high], 1), matrix, preferred_element_type=F32)


def times(real, imag, cos, sin):
    return real * cos - imag * sin, real * sin + imag * cos


def times_conj(real, imag, cos, sin):
    return real * cos + imag * sin, imag * cos - real * sin


def add(a, b):
    return a[0] + b[0], a[1] + b[1]


def sub(a, b):
    return a[0] - b[0], a[1] - b[1]


def quarter(a, sign):
    return (-a[1], a[0]) if sign > 0 else (a[1], -a[0])


def dft4(z, sign):
    e0, e1 = add(z[0], z[2]), sub(z[0], z[2])
    o0, o1 = add(z[1], z[3]), quarter(sub(z[1], z[3]), sign)
    return [add(e0, o0), add(e1, o1), sub(e0, o0), sub(e1, o1)]


def dft8(z, sign):
    even, odd = dft4(z[0::2], sign), dft4(z[1::2], sign)
    root = math.sqrt(0.5)
    q1 = quarter(odd[1], sign)
    q3 = quarter(odd[3], sign)
    odd = [
        odd[0],
        ((odd[1][0] + q1[0]) * root, (odd[1][1] + q1[1]) * root),
        quarter(odd[2], sign),
        ((q3[0] - odd[3][0]) * root, (q3[1] - odd[3][1]) * root),
    ]
    return [add(even[k], odd[k]) for k in range(4)] + [sub(even[k], odd[k]) for k in range(4)]


def sin_cos(angle):
    half = angle * 0.5
    sq = half * half
    sine = 0.0
    for power in (13, 11, 9, 7, 5, 3, 1):
        sine = sine * sq + (-1.0) ** (power // 2) / math.factorial(power)
    cosine = 0.0
    for power in (12, 10, 8, 6, 4, 2, 0):
        cosine = cosine * sq + (-1.0) ** (power // 2) / math.factorial(power)
    sine = sine * half
    return 2.0 * sine * cosine, 1.0 - 2.0 * sine * sine


def where_is(coord):
    every = slice(None)
    y = coord.get("y")
    return (
        every if y is None else y % 2,
        coord.get("x", every),
        coord.get("z", every),
        every if y is None else y // 2,
        coord.get("c", every),
    )


def device_at(coord):
    y = coord["y"]
    return ((y % 2) * 4 + coord["x"], coord["z"] * 4 + (y // 2) * 2 + coord["c"])


def slot(exchange, stage):
    return exchange * 3 + stage - 1


SLOTS = 3 * EXCHANGES - 2


def kernel(x_ref, chirp_ref, *refs):
    count = len(NAMES)
    table_refs, out_ref, refs = refs[:count], refs[count], refs[count + 1 :]
    held, refs = dict(zip(NAMES, refs[:count])), refs[count:]
    (bufs, chirp_in, response, work, lanes_work, dev_fwd, dev_inv, send_sem, recv_sem, load_sem) = refs

    row, col = lax.axis_index("row"), lax.axis_index("col")
    me = row * 16 + col
    here = {"x": row % 4, "y": row // 4 + 2 * (col // 2 % 2), "z": col // 4, "c": col % 2}

    loads = {}
    for i, (name, src) in enumerate(zip(NAMES + ("chirp",), table_refs + (chirp_ref,))):
        dst = chirp_in if name == "chirp" else held[name]
        loads[name] = pltpu.make_async_copy(src, dst, load_sem.at[i])

    def peers(axes):
        for steps in itertools.product(*[range(SIZES[a]) for a in axes]):
            there = dict(here)
            for axis, step in zip(axes, steps):
                there[axis] = (here[axis] + step) % SIZES[axis]
            yield any(steps), there

    barrier = pltpu.get_barrier_semaphore()
    greeted = [there for axes in ORDERS[0] for remote, there in peers(axes) if remote]
    for there in greeted:
        pl.semaphore_signal(barrier, inc=1, device_id=device_at(there), device_id_type=MESH)
    for name in ("roots", "shift", "chirp", "outer", "left_fwd", "inner", "small", "right_fwd", "right_inv", "left_inv"):
        loads[name].start()
    pl.semaphore_wait(barrier, len(greeted))

    def stage_ref(stream, exchange, stage):
        if exchange == 0 and stage == 0:
            return x_ref.at[stream // 2, stream % 2]
        if exchange == EXCHANGES - 1 and stage == 2:
            return out_ref.at[stream // 2, stream % 2]
        return bufs.at[stream, slot(exchange, stage)]

    def sub_ref(stream, exchange, stage, where):
        if exchange == 0 and stage == 0:
            return x_ref.at[(stream // 2,) + where + (stream % 2,)]
        if exchange == EXCHANGES - 1 and stage == 2:
            return out_ref.at[(stream // 2,) + where + (stream % 2,)]
        return bufs.at[(stream, slot(exchange, stage)) + where]

    def sem_index(exchange, phase):
        return exchange * 2 + phase

    def send(stream, exchange, phase):
        axes = ORDERS[stream][phase]
        k = sem_index(exchange, phase)
        mine = where_is({a: here[a] for a in axes})
        for remote, there in peers(axes):
            src = sub_ref(stream, exchange, phase, where_is({a: there[a] for a in axes}))
            dst = sub_ref(stream, exchange, phase + 1, mine)
            if remote:
                pltpu.make_async_remote_copy(
                    src_ref=src,
                    dst_ref=dst,
                    send_sem=send_sem.at[stream, k],
                    recv_sem=recv_sem.at[stream, k],
                    device_id=device_at(there),
                    device_id_type=MESH,
                ).start()
            else:
                pltpu.make_async_copy(src, dst, recv_sem.at[stream, k]).start()

    def arrive(stream, exchange, phase):
        whole = sub_ref(stream, exchange, phase + 1, (slice(None),) * 5)
        pltpu.make_async_copy(whole, whole, recv_sem.at[stream, sem_index(exchange, phase)]).wait()

    def sent(stream, exchange, phase):
        share = math.prod(SIZES[a] for a in ORDERS[stream][phase])
        part = bufs.at[stream, 0].reshape(128, 8, 128).at[pl.ds(0, 128 - 128 // share)]
        pltpu.make_async_copy(part, part, send_sem.at[stream, sem_index(exchange, phase)]).wait()

    def flat(stream, exchange, stage):
        return bufs.at[stream, slot(exchange, stage)].reshape(1024, 128)

    def row_of(block, part):
        return pl.ds(block % 4 * 2 + part, 128, stride=8)

    def load_pair(refs2, block):
        out = []
        for part in range(2):
            out.append(
                jnp.concatenate([refs2[b // 4][row_of(b, part), :] for b in (block, block + 1)], 1)
            )
        return out

    def build_matrices():
        for name in ("roots", "shift"):
            loads[name].wait()
        re, im = held["roots"][0], held["roots"][1]
        sre, sim = held["shift"][0], held["shift"][1]
        on_lane = lax.broadcasted_iota(jnp.int32, (128, 128), 1) == me
        on_row = lax.broadcasted_iota(jnp.int32, (128, 128), 0) == me
        pick = lambda mask, v, axis: jnp.sum(jnp.where(mask, v, 0.0), axis=axis, keepdims=True)
        fre, fim = times(re, im, pick(on_lane, sre, 1), pick(on_lane, sim, 1))
        ire, iim = times(re, im, pick(on_row, sre, 0), pick(on_row, sim, 0))
        ire, iim = ire * (1.0 / PIECES), iim * (-1.0 / PIECES)
        for ref, r, i in ((dev_fwd, fre, fim), (dev_inv, ire, iim)):
            for half, (a, b) in enumerate(((r, -i), (i, r))):
                high, low = split(jnp.concatenate([a, b], 1))
                ref[pl.ds(half * 128, 128), :] = jnp.concatenate([high, high, low], 1)

    def build_response():
        loads["chirp"].wait()
        for kb in range(BLOCKS):
            angle = chirp_in[pl.ds(kb, 128, stride=8), :].T
            sine, cosine = sin_cos(angle)
            response[kb, 0] = cosine
            response[kb, 1] = sine

    def first_step(stream):
        src, dst = flat(stream, 0, 2), flat(stream, 1, 0)
        outer = held["outer"]
        for block in range(stream % 2 * 4, stream % 2 * 4 + 4, 2):
            real, imag = load_pair((src, src), block)
            real, imag = left_product(dev_fwd[...], real, imag)
            for i in range(2):
                b = block + i
                lanes = slice(i * 128, i * 128 + 128)
                r, m = times(real[:, lanes], imag[:, lanes], outer[b, 0], outer[b, 1])
                dst[row_of(b, 0), :] = r
                dst[row_of(b, 1), :] = m

    def middle_open(stream):
        src = flat(stream, 1, 2)
        inner = held["inner"]
        for block in range(stream % 2 * 4, stream % 2 * 4 + 4, 2):
            real, imag = load_pair((src, src), block)
            real, imag = left_product(held["left_fwd"][...], real, imag)
            for i in range(2):
                b = block + i
                lanes = slice(i * 128, i * 128 + 128)
                r, m = times(real[:, lanes], imag[:, lanes], inner[b, 0], inner[b, 1])
                work[b, 0] = r
                work[b, 1] = m

    def middle_core():
        inner, small = held["inner"], held["small"]

        def forward(step, _):
            rows = pl.ds(pl.multiple_of(step * 8, 8), 8)
            z = dft8([(work[b, 0, rows, :], work[b, 1, rows, :]) for b in range(BLOCKS)], -1)
            for k in range(BLOCKS):
                r, m = z[k]
                if k:
                    r, m = times(r, m, small[k, 0:1, :], small[k, 1:2, :])
                lanes_work[k, rows, 0:128] = r
                lanes_work[k, rows, 128:256] = m
            return 0

        lax.fori_loop(0, 16, forward, 0, unroll=UNROLL_A)

        def across(step, _):
            ks = pl.ds(step * WIDE, WIDE)
            value = lanes_work[ks].reshape(WIDE * 128, 256)
            value = right_product(value, held["right_fwd"][...])
            ch = response[ks]
            cosine = ch[:, 0].reshape(WIDE * 128, 128)
            sine = ch[:, 1].reshape(WIDE * 128, 128)
            r, m = times(value[:, :128], value[:, 128:], cosine, sine)
            value = right_product(jnp.concatenate([r, m], 1), held["right_inv"][...])
            lanes_work[ks] = value.reshape(WIDE, 128, 256)
            return 0

        lax.fori_loop(0, BLOCKS // WIDE, across, 0, unroll=UNROLL_C)

        def backward(step, _):
            rows = pl.ds(pl.multiple_of(step * 8, 8), 8)
            z = []
            for k in range(BLOCKS):
                r, m = lanes_work[k, rows, 0:128], lanes_work[k, rows, 128:256]
                if k:
                    r, m = times_conj(r, m, small[k, 0:1, :], small[k, 1:2, :])
                z.append((r, m))
            z = dft8(z, 1)
            for b in range(BLOCKS):
                r, m = times_conj(z[b][0], z[b][1], inner[b, 0, rows, :], inner[b, 1, rows, :])
                work[b, 0, rows, :] = r
                work[b, 1, rows, :] = m
            return 0

        lax.fori_loop(0, 16, backward, 0, unroll=UNROLL_A)

    def middle_close(stream):
        dst = flat(stream, 2, 0)
        for block in range(stream % 2 * 4, stream % 2 * 4 + 4, 2):
            real = jnp.concatenate([work[block, 0], work[block + 1, 0]], 1)
            imag = jnp.concatenate([work[block, 1], work[block + 1, 1]], 1)
            real, imag = left_product(held["left_inv"][...], real, imag)
            for i in range(2):
                b = block + i
                lanes = slice(i * 128, i * 128 + 128)
                dst[row_of(b, 0), :] = real[:, lanes]
                dst[row_of(b, 1), :] = imag[:, lanes]

    def last_step(stream):
        src, dst = flat(stream, 2, 2), flat(stream, 3, 0)
        outer = held["outer"]
        for block in range(stream % 2 * 4, stream % 2 * 4 + 4, 2):
            parts = []
            for b in (block, block + 1):
                parts.append(times_conj(src[row_of(b, 0), :], src[row_of(b, 1), :], outer[b, 0], outer[b, 1]))
            real = jnp.concatenate([p[0] for p in parts], 1)
            imag = jnp.concatenate([p[1] for p in parts], 1)
            real, imag = left_product(dev_inv[...], real, imag)
            for i in range(2):
                b = block + i
                lanes = slice(i * 128, i * 128 + 128)
                dst[row_of(b, 0), :] = real[:, lanes]
                dst[row_of(b, 1), :] = imag[:, lanes]

    def settle(step):
        if step >= 0:
            for stream in range(STREAMS):
                sent(stream, step // 2, step % 2)

    for stream in range(STREAMS):
        send(stream, 0, 0)
    build_matrices()
    for exchange in range(EXCHANGES):
        for stream in range(STREAMS):
            arrive(stream, exchange, 0)
            send(stream, exchange, 1)
        if exchange == 0:
            build_response()
            for name in ("outer", "left_fwd", "inner", "small", "right_fwd", "right_inv", "left_inv"):
                loads[name].wait()
        settle(2 * exchange - 1)
        settle(2 * exchange)
        for pair in range(2):
            streams = (2 * pair, 2 * pair + 1)
            for stream in streams:
                arrive(stream, exchange, 1)
                if exchange == 0:
                    first_step(stream)
                if exchange == 1:
                    middle_open(stream)
                if exchange == 2:
                    last_step(stream)
                if exchange in (0, 2):
                    send(stream, exchange + 1, 0)
            if exchange == 1:
                middle_core()
                for stream in streams:
                    middle_close(stream)
                    send(stream, exchange + 1, 0)
    settle(2 * EXCHANGES - 1)


def body(voltages, chirp_phase):
    shape = (2,) + DEVICE_DIMS + (2,) + TILE
    rows = voltages.reshape(2, 2, PIECES * BLOCKS, LANES).transpose(0, 2, 1, 3).reshape(shape)
    any_space = pl.BlockSpec(memory_space=pl.ANY)
    values = [jnp.asarray(TABLES[name]) for name in NAMES]
    operands = [rows, chirp_phase.reshape(PIECES * BLOCKS, LANES)] + values
    held = [pltpu.VMEM(v.shape, v.dtype) for v in values]
    out = pl.pallas_call(
        kernel,
        out_shape=pltpu.VMEM(shape, F32),
        in_specs=[any_space] * (2 + len(values)),
        out_specs=pl.BlockSpec(memory_space=pltpu.VMEM),
        scratch_shapes=held
        + [
            pltpu.VMEM((STREAMS, SLOTS) + DEVICE_DIMS + TILE, F32),
            pltpu.VMEM((PIECES * BLOCKS, LANES), F32),
            pltpu.VMEM((BLOCKS, 2, 128, 128), F32),
            pltpu.VMEM((BLOCKS, 2, 128, 128), F32),
            pltpu.VMEM((BLOCKS, 128, 256), F32),
            pltpu.VMEM((256, 768), BF16),
            pltpu.VMEM((256, 768), BF16),
            pltpu.SemaphoreType.DMA((STREAMS, 2 * EXCHANGES)),
            pltpu.SemaphoreType.DMA((STREAMS, 2 * EXCHANGES)),
            pltpu.SemaphoreType.DMA((len(values) + 1,)),
        ],
        name="dedisperse",
        compiler_params=pltpu.CompilerParams(
            collective_id=0, has_side_effects=True, vmem_limit_bytes=48 * 1024 * 1024
        ),
        cost_estimate=pl.CostEstimate(flops=5_000_000_000, bytes_accessed=9_000_000, transcendentals=0),
    )(*[pltpu.with_memory_space_constraint(v, pltpu.HBM) for v in operands])
    return out.reshape(2, PIECES * BLOCKS, 2, LANES).transpose(0, 2, 1, 3).reshape(voltages.shape)


def solution(mesh):
    placed = (P(None, None, None, ("row", "col")), P(None, ("row", "col"), None))
    return jax.shard_map(
        body,
        mesh=mesh,
        in_specs=placed,
        out_specs=P(None, None, None, ("row", "col")),
        check_vma=False,
    )
```

```python
import itertools
import math

import jax
import jax.numpy as jnp
import ml_dtypes
import numpy as np
from jax import lax
from jax.experimental import pallas as pl
from jax.experimental.pallas import tpu as pltpu
from jax.sharding import PartitionSpec as P

MESH = pl.DeviceIdType.MESH
F32 = jnp.float32
BF16 = jnp.bfloat16
PIECES = 128
LANES = 128
BLOCKS = 8
SEG = PIECES * BLOCKS * LANES
TOTAL = PIECES * SEG
DEVICE_DIMS = (2, 4, 4, 2, 2)
TILE = (8, 128)
SIZES = {"x": 4, "y": 4, "z": 4, "c": 2}
ORDERS = (("xc", "yz"), ("yz", "xc"), ("xc", "yz"), ("yz", "xc"))
STREAMS = 4
EXCHANGES = 4
DEPTH = 16


def unit_roots(index, modulus):
    angles = -2.0 * math.pi * (index % modulus) / modulus
    return np.cos(angles), np.sin(angles)


def three_pass(matrix, axis, tall=False):
    high = matrix.astype(ml_dtypes.bfloat16)
    low = (matrix - high.astype(np.float64)).astype(ml_dtypes.bfloat16)
    return np.concatenate([high, low] if axis == 0 and tall else [high, high, low], axis)


def tables():
    idx = np.arange(128, dtype=np.int64)
    re, im = unit_roots(idx[:, None] * idx[None, :], 128)
    left = lambda r, i: np.block([[r, -i], [i, r]])
    right = lambda r, i: np.block([[r, i], [-i, r]])
    offsets = np.arange(BLOCKS * LANES, dtype=np.int64).reshape(BLOCKS, 1, LANES)
    grid = offsets * idx[None, :, None]
    kb = np.arange(BLOCKS, dtype=np.int64)
    small = kb[:, None] * idx[None, :]
    f32 = lambda pair, axis: np.stack(pair, axis).astype(np.float32)
    return {
        "roots": f32((re, im), 0),
        "shift": f32(unit_roots(idx[:, None] * idx[None, :], 16384), 0),
        "outer": f32(unit_roots(grid, TOTAL), 1),
        "inner": f32(unit_roots(grid, SEG), 1),
        "small": f32(unit_roots(small, BLOCKS * LANES), 1),
        "left_fwd": three_pass(left(re, im), 0, True),
        "left_inv": three_pass(left(re, -im) / SEG, 0, True),
        "right_fwd": three_pass(right(re, im), 0),
        "right_inv": three_pass(right(re, -im), 0),
    }


TABLES = tables()
NAMES = tuple(TABLES)


def split(value):
    high = value.astype(BF16)
    low = (value - high.astype(F32)).astype(BF16)
    return high, low


def left_product(matrix, real, imag):
    high, low = split(jnp.concatenate([real, imag], 0))
    both = jnp.dot(matrix[:512], high, preferred_element_type=F32)
    out = both[:256] + (both[256:] + jnp.dot(matrix[:256], low, preferred_element_type=F32))
    return out[:128], out[128:]


def right_product(value, matrix):
    high, low = split(value)
    return jnp.dot(jnp.concatenate([high, low, high], 1), matrix, preferred_element_type=F32)


def times(real, imag, cos, sin):
    return real * cos - imag * sin, real * sin + imag * cos


def times_conj(real, imag, cos, sin):
    return real * cos + imag * sin, imag * cos - real * sin


def add(a, b):
    return a[0] + b[0], a[1] + b[1]


def sub(a, b):
    return a[0] - b[0], a[1] - b[1]


def quarter(a, sign):
    return (-a[1], a[0]) if sign > 0 else (a[1], -a[0])


def dft4(z, sign):
    e0, e1 = add(z[0], z[2]), sub(z[0], z[2])
    o0, o1 = add(z[1], z[3]), quarter(sub(z[1], z[3]), sign)
    return [add(e0, o0), add(e1, o1), sub(e0, o0), sub(e1, o1)]


def dft8(z, sign):
    even, odd = dft4(z[0::2], sign), dft4(z[1::2], sign)
    root = math.sqrt(0.5)
    q1 = quarter(odd[1], sign)
    q3 = quarter(odd[3], sign)
    odd = [
        odd[0],
        ((odd[1][0] + q1[0]) * root, (odd[1][1] + q1[1]) * root),
        quarter(odd[2], sign),
        ((q3[0] - odd[3][0]) * root, (q3[1] - odd[3][1]) * root),
    ]
    return [add(even[k], odd[k]) for k in range(4)] + [sub(even[k], odd[k]) for k in range(4)]


def sin_cos(angle):
    half = angle * 0.5
    sq = half * half
    sine = 0.0
    for power in (13, 11, 9, 7, 5, 3, 1):
        sine = sine * sq + (-1.0) ** (power // 2) / math.factorial(power)
    cosine = 0.0
    for power in (12, 10, 8, 6, 4, 2, 0):
        cosine = cosine * sq + (-1.0) ** (power // 2) / math.factorial(power)
    sine = sine * half
    return 2.0 * sine * cosine, 1.0 - 2.0 * sine * sine


def where_is(coord):
    every = slice(None)
    y = coord.get("y")
    return (
        every if y is None else y % 2,
        coord.get("x", every),
        coord.get("z", every),
        every if y is None else y // 2,
        coord.get("c", every),
    )


def device_at(coord):
    y = coord["y"]
    return ((y % 2) * 4 + coord["x"], coord["z"] * 4 + (y // 2) * 2 + coord["c"])


def slot(exchange, stage):
    return exchange * 3 + stage - 1


SLOTS = 3 * EXCHANGES - 2


def kernel(x_ref, chirp_ref, *refs):
    count = len(NAMES)
    table_refs, out_ref, refs = refs[:count], refs[count], refs[count + 1 :]
    held, refs = dict(zip(NAMES, refs[:count])), refs[count:]
    (bufs, chirp_in, response, work, dev_fwd, dev_inv, send_sem, recv_sem, load_sem) = refs

    row, col = lax.axis_index("row"), lax.axis_index("col")
    me = row * 16 + col
    here = {"x": row % 4, "y": row // 4 + 2 * (col // 2 % 2), "z": col // 4, "c": col % 2}

    loads = {}
    for i, (name, src) in enumerate(zip(NAMES + ("chirp",), table_refs + (chirp_ref,))):
        dst = chirp_in if name == "chirp" else held[name]
        loads[name] = pltpu.make_async_copy(src, dst, load_sem.at[i])

    def peers(axes):
        for steps in itertools.product(*[range(SIZES[a]) for a in axes]):
            there = dict(here)
            for axis, step in zip(axes, steps):
                there[axis] = (here[axis] + step) % SIZES[axis]
            yield any(steps), there

    barrier = pltpu.get_barrier_semaphore()
    greeted = [there for axes in ORDERS[0] for remote, there in peers(axes) if remote]
    for there in greeted:
        pl.semaphore_signal(barrier, inc=1, device_id=device_at(there), device_id_type=MESH)
    for name in ("roots", "shift", "chirp", "outer", "left_fwd", "inner", "small", "right_fwd", "right_inv", "left_inv"):
        loads[name].start()
    pl.semaphore_wait(barrier, len(greeted))

    def stage_ref(stream, exchange, stage):
        if exchange == 0 and stage == 0:
            return x_ref.at[stream // 2, stream % 2]
        if exchange == EXCHANGES - 1 and stage == 2:
            return out_ref.at[stream // 2, stream % 2]
        return bufs.at[stream, slot(exchange, stage)]

    def sub_ref(stream, exchange, stage, where):
        if exchange == 0 and stage == 0:
            return x_ref.at[(stream // 2,) + where + (stream % 2,)]
        if exchange == EXCHANGES - 1 and stage == 2:
            return out_ref.at[(stream // 2,) + where + (stream % 2,)]
        return bufs.at[(stream, slot(exchange, stage)) + where]

    def sem_index(exchange, phase):
        return exchange * 2 + phase

    def send(stream, exchange, phase):
        axes = ORDERS[stream][phase]
        k = sem_index(exchange, phase)
        mine = where_is({a: here[a] for a in axes})
        for remote, there in peers(axes):
            src = sub_ref(stream, exchange, phase, where_is({a: there[a] for a in axes}))
            dst = sub_ref(stream, exchange, phase + 1, mine)
            if remote:
                pltpu.make_async_remote_copy(
                    src_ref=src,
                    dst_ref=dst,
                    send_sem=send_sem.at[stream, k],
                    recv_sem=recv_sem.at[stream, k],
                    device_id=device_at(there),
                    device_id_type=MESH,
                ).start()
            else:
                pltpu.make_async_copy(src, dst, recv_sem.at[stream, k]).start()

    def arrive(stream, exchange, phase):
        whole = sub_ref(stream, exchange, phase + 1, (slice(None),) * 5)
        pltpu.make_async_copy(whole, whole, recv_sem.at[stream, sem_index(exchange, phase)]).wait()

    def sent(stream, exchange, phase):
        share = math.prod(SIZES[a] for a in ORDERS[stream][phase])
        part = bufs.at[stream, 0].reshape(128, 8, 128).at[pl.ds(0, 128 - 128 // share)]
        pltpu.make_async_copy(part, part, send_sem.at[stream, sem_index(exchange, phase)]).wait()

    def flat(stream, exchange, stage):
        return bufs.at[stream, slot(exchange, stage)].reshape(1024, 128)

    def row_of(block, part):
        return pl.ds(block % 4 * 2 + part, 128, stride=8)

    def load_pair(refs2, block):
        out = []
        for part in range(2):
            out.append(
                jnp.concatenate([refs2[b // 4][row_of(b, part), :] for b in (block, block + 1)], 1)
            )
        return out

    def build_matrices():
        for name in ("roots", "shift"):
            loads[name].wait()
        re, im = held["roots"][0], held["roots"][1]
        sre, sim = held["shift"][0], held["shift"][1]
        on_lane = lax.broadcasted_iota(jnp.int32, (128, 128), 1) == me
        on_row = lax.broadcasted_iota(jnp.int32, (128, 128), 0) == me
        pick = lambda mask, v, axis: jnp.sum(jnp.where(mask, v, 0.0), axis=axis, keepdims=True)
        fre, fim = times(re, im, pick(on_lane, sre, 1), pick(on_lane, sim, 1))
        ire, iim = times(re, im, pick(on_row, sre, 0), pick(on_row, sim, 0))
        ire, iim = ire * (1.0 / PIECES), iim * (-1.0 / PIECES)
        for ref, r, i in ((dev_fwd, fre, fim), (dev_inv, ire, iim)):
            for half, (a, b) in enumerate(((r, -i), (i, r))):
                high, low = split(jnp.concatenate([a, b], 1))
                ref[pl.ds(half * 128, 128), :] = high
                ref[pl.ds(256 + half * 128, 128), :] = low

    def build_response():
        loads["chirp"].wait()
        for kb in range(BLOCKS):
            angle = chirp_in[pl.ds(kb, 128, stride=8), :].T
            sine, cosine = sin_cos(angle)
            response[kb, 0] = cosine
            response[kb, 1] = sine

    def first_step(stream):
        src, dst = flat(stream, 0, 2), flat(stream, 1, 0)
        outer = held["outer"]
        for block in range(stream % 2 * 4, stream % 2 * 4 + 4, 2):
            real, imag = load_pair((src, src), block)
            real, imag = left_product(dev_fwd[...], real, imag)
            for i in range(2):
                b = block + i
                lanes = slice(i * 128, i * 128 + 128)
                r, m = times(real[:, lanes], imag[:, lanes], outer[b, 0], outer[b, 1])
                dst[row_of(b, 0), :] = r
                dst[row_of(b, 1), :] = m

    def middle_open(stream):
        src = flat(stream, 1, 2)
        inner = held["inner"]
        for block in range(stream % 2 * 4, stream % 2 * 4 + 4, 2):
            real, imag = load_pair((src, src), block)
            real, imag = left_product(held["left_fwd"][...], real, imag)
            for i in range(2):
                b = block + i
                lanes = slice(i * 128, i * 128 + 128)
                r, m = times(real[:, lanes], imag[:, lanes], inner[b, 0], inner[b, 1])
                work[b, 0] = r
                work[b, 1] = m

    def middle_core():
        inner, small = held["inner"], held["small"]

        def part(step, _):
            rows = pl.ds(pl.multiple_of(step * DEPTH, DEPTH), DEPTH)
            z = dft8([(work[b, 0, rows, :], work[b, 1, rows, :]) for b in range(BLOCKS)], -1)
            for k in range(1, BLOCKS):
                z[k] = times(z[k][0], z[k][1], small[k, 0:1, :], small[k, 1:2, :])
            value = jnp.concatenate([jnp.concatenate(pair, 1) for pair in z], 0)
            value = right_product(value, held["right_fwd"][...])
            z = []
            for k in range(BLOCKS):
                at = slice(k * DEPTH, k * DEPTH + DEPTH)
                z.append(times(value[at, :128], value[at, 128:], response[k, 0, rows, :], response[k, 1, rows, :]))
            value = jnp.concatenate([jnp.concatenate(pair, 1) for pair in z], 0)
            value = right_product(value, held["right_inv"][...])
            z = []
            for k in range(BLOCKS):
                at = slice(k * DEPTH, k * DEPTH + DEPTH)
                r, m = value[at, :128], value[at, 128:]
                z.append(times_conj(r, m, small[k, 0:1, :], small[k, 1:2, :]) if k else (r, m))
            z = dft8(z, 1)
            for b in range(BLOCKS):
                r, m = times_conj(z[b][0], z[b][1], inner[b, 0, rows, :], inner[b, 1, rows, :])
                work[b, 0, rows, :] = r
                work[b, 1, rows, :] = m
            return 0

        lax.fori_loop(0, 128 // DEPTH, part, 0, unroll=True)

    def middle_close(stream):
        dst = flat(stream, 2, 0)
        for block in range(stream % 2 * 4, stream % 2 * 4 + 4, 2):
            real = jnp.concatenate([work[block, 0], work[block + 1, 0]], 1)
            imag = jnp.concatenate([work[block, 1], work[block + 1, 1]], 1)
            real, imag = left_product(held["left_inv"][...], real, imag)
            for i in range(2):
                b = block + i
                lanes = slice(i * 128, i * 128 + 128)
                dst[row_of(b, 0), :] = real[:, lanes]
                dst[row_of(b, 1), :] = imag[:, lanes]

    def last_step(stream):
        src, dst = flat(stream, 2, 2), flat(stream, 3, 0)
        outer = held["outer"]
        for block in range(stream % 2 * 4, stream % 2 * 4 + 4, 2):
            parts = []
            for b in (block, block + 1):
                parts.append(times_conj(src[row_of(b, 0), :], src[row_of(b, 1), :], outer[b, 0], outer[b, 1]))
            real = jnp.concatenate([p[0] for p in parts], 1)
            imag = jnp.concatenate([p[1] for p in parts], 1)
            real, imag = left_product(dev_inv[...], real, imag)
            for i in range(2):
                b = block + i
                lanes = slice(i * 128, i * 128 + 128)
                dst[row_of(b, 0), :] = real[:, lanes]
                dst[row_of(b, 1), :] = imag[:, lanes]

    def settle(step):
        if step >= 0:
            for stream in range(STREAMS):
                sent(stream, step // 2, step % 2)

    for stream in range(STREAMS):
        send(stream, 0, 0)
    build_matrices()
    for exchange in range(EXCHANGES):
        for stream in range(STREAMS):
            arrive(stream, exchange, 0)
            send(stream, exchange, 1)
        if exchange == 0:
            build_response()
            for name in ("outer", "left_fwd", "inner", "small", "right_fwd", "right_inv", "left_inv"):
                loads[name].wait()
        settle(2 * exchange - 1)
        settle(2 * exchange)
        for pair in range(2):
            streams = (2 * pair, 2 * pair + 1)
            for stream in streams:
                arrive(stream, exchange, 1)
                if exchange == 0:
                    first_step(stream)
                if exchange == 1:
                    middle_open(stream)
                if exchange == 2:
                    last_step(stream)
                if exchange in (0, 2):
                    send(stream, exchange + 1, 0)
            if exchange == 1:
                middle_core()
                for stream in streams:
                    middle_close(stream)
                    send(stream, exchange + 1, 0)
    settle(2 * EXCHANGES - 1)


def body(voltages, chirp_phase):
    shape = (2,) + DEVICE_DIMS + (2,) + TILE
    rows = voltages.reshape(2, 2, PIECES * BLOCKS, LANES).transpose(0, 2, 1, 3).reshape(shape)
    any_space = pl.BlockSpec(memory_space=pl.ANY)
    values = [jnp.asarray(TABLES[name]) for name in NAMES]
    operands = [rows, chirp_phase.reshape(PIECES * BLOCKS, LANES)] + values
    held = [pltpu.VMEM(v.shape, v.dtype) for v in values]
    out = pl.pallas_call(
        kernel,
        out_shape=pltpu.VMEM(shape, F32),
        in_specs=[any_space] * (2 + len(values)),
        out_specs=pl.BlockSpec(memory_space=pltpu.VMEM),
        scratch_shapes=held
        + [
            pltpu.VMEM((STREAMS, SLOTS) + DEVICE_DIMS + TILE, F32),
            pltpu.VMEM((PIECES * BLOCKS, LANES), F32),
            pltpu.VMEM((BLOCKS, 2, 128, 128), F32),
            pltpu.VMEM((BLOCKS, 2, 128, 128), F32),
            pltpu.VMEM((512, 256), BF16),
            pltpu.VMEM((512, 256), BF16),
            pltpu.SemaphoreType.DMA((STREAMS, 2 * EXCHANGES)),
            pltpu.SemaphoreType.DMA((STREAMS, 2 * EXCHANGES)),
            pltpu.SemaphoreType.DMA((len(values) + 1,)),
        ],
        name="dedisperse",
        compiler_params=pltpu.CompilerParams(
            collective_id=0, has_side_effects=True, vmem_limit_bytes=48 * 1024 * 1024
        ),
        cost_estimate=pl.CostEstimate(flops=5_000_000_000, bytes_accessed=9_000_000, transcendentals=0),
    )(*[pltpu.with_memory_space_constraint(v, pltpu.HBM) for v in operands])
    return out.reshape(2, PIECES * BLOCKS, 2, LANES).transpose(0, 2, 1, 3).reshape(voltages.shape)


def solution(mesh):
    placed = (P(None, None, None, ("row", "col")), P(None, ("row", "col"), None))
    return jax.shard_map(
        body,
        mesh=mesh,
        in_specs=placed,
        out_specs=P(None, None, None, ("row", "col")),
        check_vma=False,
    )
```

```python
import math

import jax
import jax.numpy as jnp
import ml_dtypes
import numpy as np
from jax import lax
from jax.experimental import pallas as pl
from jax.experimental.pallas import tpu as pltpu
from jax.sharding import PartitionSpec as P

MESH = pl.DeviceIdType.MESH
F32 = jnp.float32
BF16 = jnp.bfloat16
PIECES = 128
LANES = 128
BLOCKS = 8
SEG = PIECES * BLOCKS * LANES
TOTAL = PIECES * SEG
DEVICE_DIMS = (2, 4, 4, 2, 2)
TILE = (8, 128)
SIZES = {"x": 4, "y": 4, "z": 4, "c": 2}
ORDERS = (("xc", "yz"), ("yz", "xc"), ("xc", "yz"), ("yz", "xc"))
STREAMS = 4
STEPS = {
    "xc": ((1, 1), (3, 1), (2, 0), (2, 1), (1, 0), (3, 0), (0, 1), (0, 0)),
    "yz": (
        ((2, 2), (3, 2), (2, 1), (2, 3), (1, 2), (0, 2), (3, 1), (3, 3))
        + ((2, 0), (1, 1), (1, 3), (0, 1), (0, 3), (3, 0), (1, 0), (0, 0))
    ),
}
EXCHANGES = 4
DEPTH = 16


def unit_roots(index, modulus):
    angles = -2.0 * math.pi * (index % modulus) / modulus
    return np.cos(angles), np.sin(angles)


def three_pass(matrix, axis, tall=False):
    high = matrix.astype(ml_dtypes.bfloat16)
    low = (matrix - high.astype(np.float64)).astype(ml_dtypes.bfloat16)
    return np.concatenate([high, low] if axis == 0 and tall else [high, high, low], axis)


def tables():
    idx = np.arange(128, dtype=np.int64)
    re, im = unit_roots(idx[:, None] * idx[None, :], 128)
    left = lambda r, i: np.block([[r, -i], [i, r]])
    right = lambda r, i: np.block([[r, i], [-i, r]])
    offsets = np.arange(BLOCKS * LANES, dtype=np.int64).reshape(BLOCKS, 1, LANES)
    grid = offsets * idx[None, :, None]
    kb = np.arange(BLOCKS, dtype=np.int64)
    small = kb[:, None] * idx[None, :]
    f32 = lambda pair, axis: np.stack(pair, axis).astype(np.float32)
    return {
        "roots": f32((re, im), 0),
        "shift": f32(unit_roots(idx[:, None] * idx[None, :], 16384), 0),
        "outer": f32(unit_roots(grid, TOTAL), 1),
        "inner": f32(unit_roots(grid, SEG), 1),
        "small": f32(unit_roots(small, BLOCKS * LANES), 1),
        "left_fwd": three_pass(left(re, im), 0, True),
        "left_inv": three_pass(left(re, -im) / SEG, 0, True),
        "right_fwd": three_pass(right(re, im), 0),
        "right_inv": three_pass(right(re, -im), 0),
    }


TABLES = tables()
NAMES = tuple(TABLES)


def split(value):
    high = value.astype(BF16)
    low = (value - high.astype(F32)).astype(BF16)
    return high, low


def left_product(matrix, real, imag):
    high, low = split(jnp.concatenate([real, imag], 0))
    both = jnp.dot(matrix[:512], high, preferred_element_type=F32)
    out = both[:256] + (both[256:] + jnp.dot(matrix[:256], low, preferred_element_type=F32))
    return out[:128], out[128:]


def right_product(value, matrix):
    high, low = split(value)
    return jnp.dot(jnp.concatenate([high, low, high], 1), matrix, preferred_element_type=F32)


def times(real, imag, cos, sin):
    return real * cos - imag * sin, real * sin + imag * cos


def times_conj(real, imag, cos, sin):
    return real * cos + imag * sin, imag * cos - real * sin


def add(a, b):
    return a[0] + b[0], a[1] + b[1]


def sub(a, b):
    return a[0] - b[0], a[1] - b[1]


def quarter(a, sign):
    return (-a[1], a[0]) if sign > 0 else (a[1], -a[0])


def dft4(z, sign):
    e0, e1 = add(z[0], z[2]), sub(z[0], z[2])
    o0, o1 = add(z[1], z[3]), quarter(sub(z[1], z[3]), sign)
    return [add(e0, o0), add(e1, o1), sub(e0, o0), sub(e1, o1)]


def dft8(z, sign):
    even, odd = dft4(z[0::2], sign), dft4(z[1::2], sign)
    root = math.sqrt(0.5)
    q1 = quarter(odd[1], sign)
    q3 = quarter(odd[3], sign)
    odd = [
        odd[0],
        ((odd[1][0] + q1[0]) * root, (odd[1][1] + q1[1]) * root),
        quarter(odd[2], sign),
        ((q3[0] - odd[3][0]) * root, (q3[1] - odd[3][1]) * root),
    ]
    return [add(even[k], odd[k]) for k in range(4)] + [sub(even[k], odd[k]) for k in range(4)]


def sin_cos(angle):
    half = angle * 0.5
    sq = half * half
    sine = 0.0
    for power in (13, 11, 9, 7, 5, 3, 1):
        sine = sine * sq + (-1.0) ** (power // 2) / math.factorial(power)
    cosine = 0.0
    for power in (12, 10, 8, 6, 4, 2, 0):
        cosine = cosine * sq + (-1.0) ** (power // 2) / math.factorial(power)
    sine = sine * half
    return 2.0 * sine * cosine, 1.0 - 2.0 * sine * sine


def where_is(coord):
    every = slice(None)
    y = coord.get("y")
    return (
        every if y is None else y % 2,
        coord.get("x", every),
        coord.get("z", every),
        every if y is None else y // 2,
        coord.get("c", every),
    )


def device_at(coord):
    y = coord["y"]
    return ((y % 2) * 4 + coord["x"], coord["z"] * 4 + (y // 2) * 2 + coord["c"])


def slot(exchange, stage):
    return exchange * 3 + stage - 1


SLOTS = 3 * EXCHANGES - 2


def kernel(x_ref, chirp_ref, *refs):
    count = len(NAMES)
    table_refs, out_ref, refs = refs[:count], refs[count], refs[count + 1 :]
    held, refs = dict(zip(NAMES, refs[:count])), refs[count:]
    (bufs, chirp_in, response, work, dev_fwd, dev_inv, send_sem, recv_sem, load_sem) = refs

    row, col = lax.axis_index("row"), lax.axis_index("col")
    me = row * 16 + col
    here = {"x": row % 4, "y": row // 4 + 2 * (col // 2 % 2), "z": col // 4, "c": col % 2}

    loads = {}
    for i, (name, src) in enumerate(zip(NAMES + ("chirp",), table_refs + (chirp_ref,))):
        dst = chirp_in if name == "chirp" else held[name]
        loads[name] = pltpu.make_async_copy(src, dst, load_sem.at[i])

    def peers(axes, mirror=False):
        for steps in STEPS[axes]:
            if mirror:
                steps = tuple(-step % SIZES[axis] for axis, step in zip(axes, steps))
            there = dict(here)
            for axis, step in zip(axes, steps):
                there[axis] = (here[axis] + step) % SIZES[axis]
            yield any(steps), there

    barrier = pltpu.get_barrier_semaphore()
    greeted = [there for axes in ORDERS[0] for remote, there in peers(axes) if remote]
    for there in greeted:
        pl.semaphore_signal(barrier, inc=1, device_id=device_at(there), device_id_type=MESH)
    for name in ("roots", "shift", "chirp", "outer", "left_fwd", "inner", "small", "right_fwd", "right_inv", "left_inv"):
        loads[name].start()
    pl.semaphore_wait(barrier, len(greeted))

    def stage_ref(stream, exchange, stage):
        if exchange == 0 and stage == 0:
            return x_ref.at[stream // 2, stream % 2]
        if exchange == EXCHANGES - 1 and stage == 2:
            return out_ref.at[stream // 2, stream % 2]
        return bufs.at[stream, slot(exchange, stage)]

    def sub_ref(stream, exchange, stage, where):
        if exchange == 0 and stage == 0:
            return x_ref.at[(stream // 2,) + where + (stream % 2,)]
        if exchange == EXCHANGES - 1 and stage == 2:
            return out_ref.at[(stream // 2,) + where + (stream % 2,)]
        return bufs.at[(stream, slot(exchange, stage)) + where]

    def sem_index(exchange, phase):
        return exchange * 2 + phase

    def send(stream, exchange, phase):
        axes = ORDERS[stream][phase]
        k = sem_index(exchange, phase)
        mine = where_is({a: here[a] for a in axes})
        for remote, there in peers(axes, stream >= 2):
            src = sub_ref(stream, exchange, phase, where_is({a: there[a] for a in axes}))
            dst = sub_ref(stream, exchange, phase + 1, mine)
            if remote:
                pltpu.make_async_remote_copy(
                    src_ref=src,
                    dst_ref=dst,
                    send_sem=send_sem.at[stream, k],
                    recv_sem=recv_sem.at[stream, k],
                    device_id=device_at(there),
                    device_id_type=MESH,
                ).start()
            else:
                pltpu.make_async_copy(src, dst, recv_sem.at[stream, k]).start()

    def arrive(stream, exchange, phase):
        whole = sub_ref(stream, exchange, phase + 1, (slice(None),) * 5)
        pltpu.make_async_copy(whole, whole, recv_sem.at[stream, sem_index(exchange, phase)]).wait()

    def sent(stream, exchange, phase):
        share = math.prod(SIZES[a] for a in ORDERS[stream][phase])
        part = bufs.at[stream, 0].reshape(128, 8, 128).at[pl.ds(0, 128 - 128 // share)]
        pltpu.make_async_copy(part, part, send_sem.at[stream, sem_index(exchange, phase)]).wait()

    def flat(stream, exchange, stage):
        return bufs.at[stream, slot(exchange, stage)].reshape(1024, 128)

    def row_of(block, part):
        return pl.ds(block % 4 * 2 + part, 128, stride=8)

    def load_pair(refs2, block):
        out = []
        for part in range(2):
            out.append(
                jnp.concatenate([refs2[b // 4][row_of(b, part), :] for b in (block, block + 1)], 1)
            )
        return out

    def build_matrices():
        for name in ("roots", "shift"):
            loads[name].wait()
        re, im = held["roots"][0], held["roots"][1]
        sre, sim = held["shift"][0], held["shift"][1]
        on_lane = lax.broadcasted_iota(jnp.int32, (128, 128), 1) == me
        on_row = lax.broadcasted_iota(jnp.int32, (128, 128), 0) == me
        pick = lambda mask, v, axis: jnp.sum(jnp.where(mask, v, 0.0), axis=axis, keepdims=True)
        fre, fim = times(re, im, pick(on_lane, sre, 1), pick(on_lane, sim, 1))
        ire, iim = times(re, im, pick(on_row, sre, 0), pick(on_row, sim, 0))
        ire, iim = ire * (1.0 / PIECES), iim * (-1.0 / PIECES)
        for ref, r, i in ((dev_fwd, fre, fim), (dev_inv, ire, iim)):
            for half, (a, b) in enumerate(((r, -i), (i, r))):
                high, low = split(jnp.concatenate([a, b], 1))
                ref[pl.ds(half * 128, 128), :] = high
                ref[pl.ds(256 + half * 128, 128), :] = low

    def build_response():
        loads["chirp"].wait()
        for kb in range(BLOCKS):
            angle = chirp_in[pl.ds(kb, 128, stride=8), :].T
            sine, cosine = sin_cos(angle)
            response[kb, 0] = cosine
            response[kb, 1] = sine

    def first_step(stream):
        src, dst = flat(stream, 0, 2), flat(stream, 1, 0)
        outer = held["outer"]
        for block in range(stream % 2 * 4, stream % 2 * 4 + 4, 2):
            real, imag = load_pair((src, src), block)
            real, imag = left_product(dev_fwd[...], real, imag)
            for i in range(2):
                b = block + i
                lanes = slice(i * 128, i * 128 + 128)
                r, m = times(real[:, lanes], imag[:, lanes], outer[b, 0], outer[b, 1])
                dst[row_of(b, 0), :] = r
                dst[row_of(b, 1), :] = m

    def middle_open(stream):
        src = flat(stream, 1, 2)
        inner = held["inner"]
        for block in range(stream % 2 * 4, stream % 2 * 4 + 4, 2):
            real, imag = load_pair((src, src), block)
            real, imag = left_product(held["left_fwd"][...], real, imag)
            for i in range(2):
                b = block + i
                lanes = slice(i * 128, i * 128 + 128)
                r, m = times(real[:, lanes], imag[:, lanes], inner[b, 0], inner[b, 1])
                work[b, 0] = r
                work[b, 1] = m

    def middle_core():
        inner, small = held["inner"], held["small"]

        def part(step, _):
            rows = pl.ds(pl.multiple_of(step * DEPTH, DEPTH), DEPTH)
            z = dft8([(work[b, 0, rows, :], work[b, 1, rows, :]) for b in range(BLOCKS)], -1)
            for k in range(1, BLOCKS):
                z[k] = times(z[k][0], z[k][1], small[k, 0:1, :], small[k, 1:2, :])
            value = jnp.concatenate([jnp.concatenate(pair, 1) for pair in z], 0)
            value = right_product(value, held["right_fwd"][...])
            z = []
            for k in range(BLOCKS):
                at = slice(k * DEPTH, k * DEPTH + DEPTH)
                z.append(times(value[at, :128], value[at, 128:], response[k, 0, rows, :], response[k, 1, rows, :]))
            value = jnp.concatenate([jnp.concatenate(pair, 1) for pair in z], 0)
            value = right_product(value, held["right_inv"][...])
            z = []
            for k in range(BLOCKS):
                at = slice(k * DEPTH, k * DEPTH + DEPTH)
                r, m = value[at, :128], value[at, 128:]
                z.append(times_conj(r, m, small[k, 0:1, :], small[k, 1:2, :]) if k else (r, m))
            z = dft8(z, 1)
            for b in range(BLOCKS):
                r, m = times_conj(z[b][0], z[b][1], inner[b, 0, rows, :], inner[b, 1, rows, :])
                work[b, 0, rows, :] = r
                work[b, 1, rows, :] = m
            return 0

        lax.fori_loop(0, 128 // DEPTH, part, 0, unroll=True)

    def middle_close(stream):
        dst = flat(stream, 2, 0)
        for block in range(stream % 2 * 4, stream % 2 * 4 + 4, 2):
            real = jnp.concatenate([work[block, 0], work[block + 1, 0]], 1)
            imag = jnp.concatenate([work[block, 1], work[block + 1, 1]], 1)
            real, imag = left_product(held["left_inv"][...], real, imag)
            for i in range(2):
                b = block + i
                lanes = slice(i * 128, i * 128 + 128)
                dst[row_of(b, 0), :] = real[:, lanes]
                dst[row_of(b, 1), :] = imag[:, lanes]

    def last_step(stream):
        src, dst = flat(stream, 2, 2), flat(stream, 3, 0)
        outer = held["outer"]
        for block in range(stream % 2 * 4, stream % 2 * 4 + 4, 2):
            parts = []
            for b in (block, block + 1):
                parts.append(times_conj(src[row_of(b, 0), :], src[row_of(b, 1), :], outer[b, 0], outer[b, 1]))
            real = jnp.concatenate([p[0] for p in parts], 1)
            imag = jnp.concatenate([p[1] for p in parts], 1)
            real, imag = left_product(dev_inv[...], real, imag)
            for i in range(2):
                b = block + i
                lanes = slice(i * 128, i * 128 + 128)
                dst[row_of(b, 0), :] = real[:, lanes]
                dst[row_of(b, 1), :] = imag[:, lanes]

    def settle(step):
        if step >= 0:
            for stream in range(STREAMS):
                sent(stream, step // 2, step % 2)

    for stream in (0, 1):
        send(stream, 0, 0)
    build_matrices()
    for stream in (2, 3):
        send(stream, 0, 0)
    for exchange in range(EXCHANGES):
        for stream in range(STREAMS):
            arrive(stream, exchange, 0)
            send(stream, exchange, 1)
        if exchange == 0:
            build_response()
            for name in ("outer", "left_fwd", "inner", "small", "right_fwd", "right_inv", "left_inv"):
                loads[name].wait()
        settle(2 * exchange - 1)
        settle(2 * exchange)
        for pair in range(2):
            streams = (2 * pair, 2 * pair + 1)
            for stream in streams:
                arrive(stream, exchange, 1)
                if exchange == 0:
                    first_step(stream)
                if exchange == 1:
                    middle_open(stream)
                if exchange == 2:
                    last_step(stream)
                if exchange in (0, 2):
                    send(stream, exchange + 1, 0)
            if exchange == 1:
                middle_core()
                for stream in streams:
                    middle_close(stream)
                    send(stream, exchange + 1, 0)
    settle(2 * EXCHANGES - 1)


def body(voltages, chirp_phase):
    shape = (2,) + DEVICE_DIMS + (2,) + TILE
    rows = voltages.reshape(2, 2, PIECES * BLOCKS, LANES).transpose(0, 2, 1, 3).reshape(shape)
    any_space = pl.BlockSpec(memory_space=pl.ANY)
    values = [jnp.asarray(TABLES[name]) for name in NAMES]
    operands = [rows, chirp_phase.reshape(PIECES * BLOCKS, LANES)] + values
    held = [pltpu.VMEM(v.shape, v.dtype) for v in values]
    out = pl.pallas_call(
        kernel,
        out_shape=pltpu.VMEM(shape, F32),
        in_specs=[any_space] * (2 + len(values)),
        out_specs=pl.BlockSpec(memory_space=pltpu.VMEM),
        scratch_shapes=held
        + [
            pltpu.VMEM((STREAMS, SLOTS) + DEVICE_DIMS + TILE, F32),
            pltpu.VMEM((PIECES * BLOCKS, LANES), F32),
            pltpu.VMEM((BLOCKS, 2, 128, 128), F32),
            pltpu.VMEM((BLOCKS, 2, 128, 128), F32),
            pltpu.VMEM((512, 256), BF16),
            pltpu.VMEM((512, 256), BF16),
            pltpu.SemaphoreType.DMA((STREAMS, 2 * EXCHANGES)),
            pltpu.SemaphoreType.DMA((STREAMS, 2 * EXCHANGES)),
            pltpu.SemaphoreType.DMA((len(values) + 1,)),
        ],
        name="dedisperse",
        compiler_params=pltpu.CompilerParams(
            collective_id=0, has_side_effects=True, vmem_limit_bytes=48 * 1024 * 1024
        ),
        cost_estimate=pl.CostEstimate(flops=5_000_000_000, bytes_accessed=9_000_000, transcendentals=0),
    )(*[pltpu.with_memory_space_constraint(v, pltpu.HBM) for v in operands])
    return out.reshape(2, PIECES * BLOCKS, 2, LANES).transpose(0, 2, 1, 3).reshape(voltages.shape)


def solution(mesh):
    placed = (P(None, None, None, ("row", "col")), P(None, ("row", "col"), None))
    return jax.shard_map(
        body,
        mesh=mesh,
        in_specs=placed,
        out_specs=P(None, None, None, ("row", "col")),
        check_vma=False,
    )
```

```python
import math

import jax
import jax.numpy as jnp
import ml_dtypes
import numpy as np
from jax import lax
from jax.experimental import pallas as pl
from jax.experimental.pallas import tpu as pltpu
from jax.sharding import PartitionSpec as P

MESH = pl.DeviceIdType.MESH
F32 = jnp.float32
BF16 = jnp.bfloat16
PIECES = 128
LANES = 128
BLOCKS = 8
SEG = PIECES * BLOCKS * LANES
TOTAL = PIECES * SEG
DEVICE_DIMS = (2, 4, 4, 2, 2)
TILE = (8, 128)
SIZES = {"x": 4, "y": 4, "z": 4, "c": 2}
ORDERS = (("xc", "yz"), ("yz", "xc"), ("xc", "yz"), ("yz", "xc"))
STREAMS = 4
STEPS = {
    "xc": ((1, 1), (3, 1), (2, 0), (2, 1), (1, 0), (3, 0), (0, 1), (0, 0)),
    "yz": (
        ((2, 2), (3, 2), (2, 1), (2, 3), (1, 2), (0, 2), (3, 1), (3, 3))
        + ((2, 0), (1, 1), (1, 3), (0, 1), (0, 3), (3, 0), (1, 0), (0, 0))
    ),
}
EXCHANGES = 4
DEPTH = 16


def unit_roots(index, modulus):
    angles = -2.0 * math.pi * (index % modulus) / modulus
    return np.cos(angles), np.sin(angles)


def three_pass(matrix, axis, tall=False):
    high = matrix.astype(ml_dtypes.bfloat16)
    low = (matrix - high.astype(np.float64)).astype(ml_dtypes.bfloat16)
    return np.concatenate([high, low] if axis == 0 and tall else [high, high, low], axis)


def tables():
    idx = np.arange(128, dtype=np.int64)
    re, im = unit_roots(idx[:, None] * idx[None, :], 128)
    left = lambda r, i: np.block([[r, -i], [i, r]])
    right = lambda r, i: np.block([[r, i], [-i, r]])
    offsets = np.arange(BLOCKS * LANES, dtype=np.int64).reshape(BLOCKS, 1, LANES)
    grid = offsets * idx[None, :, None]
    kb = np.arange(BLOCKS, dtype=np.int64)
    small = kb[:, None] * idx[None, :]
    f32 = lambda pair, axis: np.stack(pair, axis).astype(np.float32)
    return {
        "roots": f32((re, im), 0),
        "shift": f32(unit_roots(idx[:, None] * idx[None, :], 16384), 0),
        "outer": f32(unit_roots(grid, TOTAL), 1),
        "inner": f32(unit_roots(grid, SEG), 1),
        "small": f32(unit_roots(small, BLOCKS * LANES), 1),
        "left_fwd": three_pass(left(re, im), 0, True),
        "left_inv": three_pass(left(re, -im) / SEG, 0, True),
        "right_fwd": three_pass(right(re, im), 0),
        "right_inv": three_pass(right(re, -im), 0),
    }


TABLES = tables()
NAMES = tuple(TABLES)


def split(value):
    high = value.astype(BF16)
    low = (value - high.astype(F32)).astype(BF16)
    return high, low


def left_product(matrix, real, imag):
    high, low = split(jnp.concatenate([real, imag], 0))
    both = jnp.dot(matrix[:512], high, preferred_element_type=F32)
    out = both[:256] + (both[256:] + jnp.dot(matrix[:256], low, preferred_element_type=F32))
    return out[:128], out[128:]


def right_product(value, matrix):
    high, low = split(value)
    return jnp.dot(jnp.concatenate([high, low, high], 1), matrix, preferred_element_type=F32)


def times(real, imag, cos, sin):
    return real * cos - imag * sin, real * sin + imag * cos


def times_conj(real, imag, cos, sin):
    return real * cos + imag * sin, imag * cos - real * sin


def add(a, b):
    return a[0] + b[0], a[1] + b[1]


def sub(a, b):
    return a[0] - b[0], a[1] - b[1]


def quarter(a, sign):
    return (-a[1], a[0]) if sign > 0 else (a[1], -a[0])


def dft4(z, sign):
    e0, e1 = add(z[0], z[2]), sub(z[0], z[2])
    o0, o1 = add(z[1], z[3]), quarter(sub(z[1], z[3]), sign)
    return [add(e0, o0), add(e1, o1), sub(e0, o0), sub(e1, o1)]


def dft8(z, sign):
    even, odd = dft4(z[0::2], sign), dft4(z[1::2], sign)
    root = math.sqrt(0.5)
    q1 = quarter(odd[1], sign)
    q3 = quarter(odd[3], sign)
    odd = [
        odd[0],
        ((odd[1][0] + q1[0]) * root, (odd[1][1] + q1[1]) * root),
        quarter(odd[2], sign),
        ((q3[0] - odd[3][0]) * root, (q3[1] - odd[3][1]) * root),
    ]
    return [add(even[k], odd[k]) for k in range(4)] + [sub(even[k], odd[k]) for k in range(4)]


def sin_cos(angle):
    half = angle * 0.5
    sq = half * half
    sine = 0.0
    for power in (13, 11, 9, 7, 5, 3, 1):
        sine = sine * sq + (-1.0) ** (power // 2) / math.factorial(power)
    cosine = 0.0
    for power in (12, 10, 8, 6, 4, 2, 0):
        cosine = cosine * sq + (-1.0) ** (power // 2) / math.factorial(power)
    sine = sine * half
    return 2.0 * sine * cosine, 1.0 - 2.0 * sine * sine


def where_is(coord):
    every = slice(None)
    y = coord.get("y")
    return (
        every if y is None else y % 2,
        coord.get("x", every),
        coord.get("z", every),
        every if y is None else y // 2,
        coord.get("c", every),
    )


def device_at(coord):
    y = coord["y"]
    return ((y % 2) * 4 + coord["x"], coord["z"] * 4 + (y // 2) * 2 + coord["c"])


def slot(exchange, stage):
    return exchange * 3 + stage - 1


SLOTS = 3 * EXCHANGES - 2


def kernel(x_ref, chirp_ref, *refs):
    count = len(NAMES)
    table_refs, out_ref, refs = refs[:count], refs[count], refs[count + 1 :]
    held, refs = dict(zip(NAMES, refs[:count])), refs[count:]
    (bufs, chirp_in, response, work, dev_fwd, dev_inv, send_sem, recv_sem, load_sem) = refs

    row, col = lax.axis_index("row"), lax.axis_index("col")
    me = row * 16 + col
    here = {"x": row % 4, "y": row // 4 + 2 * (col // 2 % 2), "z": col // 4, "c": col % 2}

    loads = {}
    for i, (name, src) in enumerate(zip(NAMES + ("chirp",), table_refs + (chirp_ref,))):
        dst = chirp_in if name == "chirp" else held[name]
        loads[name] = pltpu.make_async_copy(src, dst, load_sem.at[i])

    def peers(axes, mirror=False):
        for steps in STEPS[axes]:
            if mirror:
                steps = tuple(-step % SIZES[axis] for axis, step in zip(axes, steps))
            there = dict(here)
            for axis, step in zip(axes, steps):
                there[axis] = (here[axis] + step) % SIZES[axis]
            yield any(steps), there

    barrier = pltpu.get_barrier_semaphore()
    greeted = [there for axes in ORDERS[0] for remote, there in peers(axes) if remote]
    for there in greeted:
        pl.semaphore_signal(barrier, inc=1, device_id=device_at(there), device_id_type=MESH)
    pl.semaphore_wait(barrier, len(greeted))

    def stage_ref(stream, exchange, stage):
        if exchange == 0 and stage == 0:
            return x_ref.at[stream // 2, stream % 2]
        if exchange == EXCHANGES - 1 and stage == 2:
            return out_ref.at[stream // 2, stream % 2]
        return bufs.at[stream, slot(exchange, stage)]

    def sub_ref(stream, exchange, stage, where):
        if exchange == 0 and stage == 0:
            return x_ref.at[(stream // 2,) + where + (stream % 2,)]
        if exchange == EXCHANGES - 1 and stage == 2:
            return out_ref.at[(stream // 2,) + where + (stream % 2,)]
        return bufs.at[(stream, slot(exchange, stage)) + where]

    def sem_index(exchange, phase):
        return exchange * 2 + phase

    def send(stream, exchange, phase):
        axes = ORDERS[stream][phase]
        k = sem_index(exchange, phase)
        mine = where_is({a: here[a] for a in axes})
        for remote, there in peers(axes, stream >= 2):
            src = sub_ref(stream, exchange, phase, where_is({a: there[a] for a in axes}))
            dst = sub_ref(stream, exchange, phase + 1, mine)
            if remote:
                pltpu.make_async_remote_copy(
                    src_ref=src,
                    dst_ref=dst,
                    send_sem=send_sem.at[stream, k],
                    recv_sem=recv_sem.at[stream, k],
                    device_id=device_at(there),
                    device_id_type=MESH,
                ).start()
            else:
                pltpu.make_async_copy(src, dst, recv_sem.at[stream, k]).start()

    def arrive(stream, exchange, phase):
        whole = sub_ref(stream, exchange, phase + 1, (slice(None),) * 5)
        pltpu.make_async_copy(whole, whole, recv_sem.at[stream, sem_index(exchange, phase)]).wait()

    def sent(stream, exchange, phase):
        share = math.prod(SIZES[a] for a in ORDERS[stream][phase])
        part = bufs.at[stream, 0].reshape(128, 8, 128).at[pl.ds(0, 128 - 128 // share)]
        pltpu.make_async_copy(part, part, send_sem.at[stream, sem_index(exchange, phase)]).wait()

    def flat(stream, exchange, stage):
        return bufs.at[stream, slot(exchange, stage)].reshape(1024, 128)

    def row_of(block, part):
        return pl.ds(block % 4 * 2 + part, 128, stride=8)

    def load_pair(refs2, block):
        out = []
        for part in range(2):
            out.append(
                jnp.concatenate([refs2[b // 4][row_of(b, part), :] for b in (block, block + 1)], 1)
            )
        return out

    def build_matrices():
        for name in ("roots", "shift"):
            loads[name].wait()
        re, im = held["roots"][0], held["roots"][1]
        sre, sim = held["shift"][0], held["shift"][1]
        on_lane = lax.broadcasted_iota(jnp.int32, (128, 128), 1) == me
        on_row = lax.broadcasted_iota(jnp.int32, (128, 128), 0) == me
        pick = lambda mask, v, axis: jnp.sum(jnp.where(mask, v, 0.0), axis=axis, keepdims=True)
        fre, fim = times(re, im, pick(on_lane, sre, 1), pick(on_lane, sim, 1))
        ire, iim = times(re, im, pick(on_row, sre, 0), pick(on_row, sim, 0))
        ire, iim = ire * (1.0 / PIECES), iim * (-1.0 / PIECES)
        for ref, r, i in ((dev_fwd, fre, fim), (dev_inv, ire, iim)):
            for half, (a, b) in enumerate(((r, -i), (i, r))):
                high, low = split(jnp.concatenate([a, b], 1))
                ref[pl.ds(half * 128, 128), :] = high
                ref[pl.ds(256 + half * 128, 128), :] = low

    def build_response():
        loads["chirp"].wait()
        for kb in range(BLOCKS):
            angle = chirp_in[pl.ds(kb, 128, stride=8), :].T
            sine, cosine = sin_cos(angle)
            response[kb, 0] = cosine
            response[kb, 1] = sine

    def first_step(stream):
        src, dst = flat(stream, 0, 2), flat(stream, 1, 0)
        outer = held["outer"]
        for block in range(stream % 2 * 4, stream % 2 * 4 + 4, 2):
            real, imag = load_pair((src, src), block)
            real, imag = left_product(dev_fwd[...], real, imag)
            for i in range(2):
                b = block + i
                lanes = slice(i * 128, i * 128 + 128)
                r, m = times(real[:, lanes], imag[:, lanes], outer[b, 0], outer[b, 1])
                dst[row_of(b, 0), :] = r
                dst[row_of(b, 1), :] = m

    def middle_open(stream):
        src = flat(stream, 1, 2)
        inner = held["inner"]
        for block in range(stream % 2 * 4, stream % 2 * 4 + 4, 2):
            real, imag = load_pair((src, src), block)
            real, imag = left_product(held["left_fwd"][...], real, imag)
            for i in range(2):
                b = block + i
                lanes = slice(i * 128, i * 128 + 128)
                r, m = times(real[:, lanes], imag[:, lanes], inner[b, 0], inner[b, 1])
                work[b, 0] = r
                work[b, 1] = m

    def middle_core():
        inner, small = held["inner"], held["small"]

        def part(step, _):
            rows = pl.ds(pl.multiple_of(step * DEPTH, DEPTH), DEPTH)
            z = dft8([(work[b, 0, rows, :], work[b, 1, rows, :]) for b in range(BLOCKS)], -1)
            for k in range(1, BLOCKS):
                z[k] = times(z[k][0], z[k][1], small[k, 0:1, :], small[k, 1:2, :])
            value = jnp.concatenate([jnp.concatenate(pair, 1) for pair in z], 0)
            value = right_product(value, held["right_fwd"][...])
            z = []
            for k in range(BLOCKS):
                at = slice(k * DEPTH, k * DEPTH + DEPTH)
                z.append(times(value[at, :128], value[at, 128:], response[k, 0, rows, :], response[k, 1, rows, :]))
            value = jnp.concatenate([jnp.concatenate(pair, 1) for pair in z], 0)
            value = right_product(value, held["right_inv"][...])
            z = []
            for k in range(BLOCKS):
                at = slice(k * DEPTH, k * DEPTH + DEPTH)
                r, m = value[at, :128], value[at, 128:]
                z.append(times_conj(r, m, small[k, 0:1, :], small[k, 1:2, :]) if k else (r, m))
            z = dft8(z, 1)
            for b in range(BLOCKS):
                r, m = times_conj(z[b][0], z[b][1], inner[b, 0, rows, :], inner[b, 1, rows, :])
                work[b, 0, rows, :] = r
                work[b, 1, rows, :] = m
            return 0

        lax.fori_loop(0, 128 // DEPTH, part, 0, unroll=True)

    def middle_close(stream):
        dst = flat(stream, 2, 0)
        for block in range(stream % 2 * 4, stream % 2 * 4 + 4, 2):
            real = jnp.concatenate([work[block, 0], work[block + 1, 0]], 1)
            imag = jnp.concatenate([work[block, 1], work[block + 1, 1]], 1)
            real, imag = left_product(held["left_inv"][...], real, imag)
            for i in range(2):
                b = block + i
                lanes = slice(i * 128, i * 128 + 128)
                dst[row_of(b, 0), :] = real[:, lanes]
                dst[row_of(b, 1), :] = imag[:, lanes]

    def last_step(stream):
        src, dst = flat(stream, 2, 2), flat(stream, 3, 0)
        outer = held["outer"]
        for block in range(stream % 2 * 4, stream % 2 * 4 + 4, 2):
            parts = []
            for b in (block, block + 1):
                parts.append(times_conj(src[row_of(b, 0), :], src[row_of(b, 1), :], outer[b, 0], outer[b, 1]))
            real = jnp.concatenate([p[0] for p in parts], 1)
            imag = jnp.concatenate([p[1] for p in parts], 1)
            real, imag = left_product(dev_inv[...], real, imag)
            for i in range(2):
                b = block + i
                lanes = slice(i * 128, i * 128 + 128)
                dst[row_of(b, 0), :] = real[:, lanes]
                dst[row_of(b, 1), :] = imag[:, lanes]

    def settle(step):
        if step >= 0:
            for stream in range(STREAMS):
                sent(stream, step // 2, step % 2)

    for stream in (0, 1):
        send(stream, 0, 0)
    for name in ("roots", "shift", "chirp", "outer", "left_fwd", "inner", "small", "right_fwd", "right_inv", "left_inv"):
        loads[name].start()
    build_matrices()
    for stream in (2, 3):
        send(stream, 0, 0)
    for exchange in range(EXCHANGES):
        for stream in range(STREAMS):
            arrive(stream, exchange, 0)
            send(stream, exchange, 1)
        if exchange == 0:
            build_response()
            for name in ("outer", "left_fwd", "inner", "small", "right_fwd", "right_inv", "left_inv"):
                loads[name].wait()
        settle(2 * exchange - 1)
        settle(2 * exchange)
        for pair in range(2):
            streams = (2 * pair, 2 * pair + 1)
            for stream in streams:
                arrive(stream, exchange, 1)
                if exchange == 0:
                    first_step(stream)
                if exchange == 1:
                    middle_open(stream)
                if exchange == 2:
                    last_step(stream)
                if exchange in (0, 2):
                    send(stream, exchange + 1, 0)
            if exchange == 1:
                middle_core()
                for stream in streams:
                    middle_close(stream)
                    send(stream, exchange + 1, 0)
    settle(2 * EXCHANGES - 1)


def body(voltages, chirp_phase):
    shape = (2,) + DEVICE_DIMS + (2,) + TILE
    rows = voltages.reshape(2, 2, PIECES * BLOCKS, LANES).transpose(0, 2, 1, 3).reshape(shape)
    any_space = pl.BlockSpec(memory_space=pl.ANY)
    values = [jnp.asarray(TABLES[name]) for name in NAMES]
    operands = [rows, chirp_phase.reshape(PIECES * BLOCKS, LANES)] + values
    held = [pltpu.VMEM(v.shape, v.dtype) for v in values]
    out = pl.pallas_call(
        kernel,
        out_shape=pltpu.VMEM(shape, F32),
        in_specs=[any_space] * (2 + len(values)),
        out_specs=pl.BlockSpec(memory_space=pltpu.VMEM),
        scratch_shapes=held
        + [
            pltpu.VMEM((STREAMS, SLOTS) + DEVICE_DIMS + TILE, F32),
            pltpu.VMEM((PIECES * BLOCKS, LANES), F32),
            pltpu.VMEM((BLOCKS, 2, 128, 128), F32),
            pltpu.VMEM((BLOCKS, 2, 128, 128), F32),
            pltpu.VMEM((512, 256), BF16),
            pltpu.VMEM((512, 256), BF16),
            pltpu.SemaphoreType.DMA((STREAMS, 2 * EXCHANGES)),
            pltpu.SemaphoreType.DMA((STREAMS, 2 * EXCHANGES)),
            pltpu.SemaphoreType.DMA((len(values) + 1,)),
        ],
        name="dedisperse",
        compiler_params=pltpu.CompilerParams(
            collective_id=0, has_side_effects=True, vmem_limit_bytes=48 * 1024 * 1024
        ),
        cost_estimate=pl.CostEstimate(flops=5_000_000_000, bytes_accessed=9_000_000, transcendentals=0),
    )(*[pltpu.with_memory_space_constraint(v, pltpu.HBM) for v in operands])
    return out.reshape(2, PIECES * BLOCKS, 2, LANES).transpose(0, 2, 1, 3).reshape(voltages.shape)


def solution(mesh):
    placed = (P(None, None, None, ("row", "col")), P(None, ("row", "col"), None))
    return jax.shard_map(
        body,
        mesh=mesh,
        in_specs=placed,
        out_specs=P(None, None, None, ("row", "col")),
        check_vma=False,
    )
```

```python
import math

import jax
import jax.numpy as jnp
import ml_dtypes
import numpy as np
from jax import lax
from jax.experimental import pallas as pl
from jax.experimental.pallas import tpu as pltpu
from jax.sharding import PartitionSpec as P

MESH = pl.DeviceIdType.MESH
F32 = jnp.float32
BF16 = jnp.bfloat16
PIECES = 128
LANES = 128
BLOCKS = 8
SEG = PIECES * BLOCKS * LANES
TOTAL = PIECES * SEG
DEVICE_DIMS = (2, 4, 4, 2, 2)
TILE = (8, 128)
SIZES = {"x": 4, "y": 4, "z": 4, "c": 2}
ORDERS = (("xc", "yz"), ("yz", "xc"), ("xc", "yz"), ("yz", "xc"))
STREAMS = 4
STEPS = {
    "xc": ((1, 1), (3, 1), (2, 0), (2, 1), (1, 0), (3, 0), (0, 1), (0, 0)),
    "yz": (
        ((2, 2), (3, 2), (2, 1), (2, 3), (1, 2), (0, 2), (3, 1), (3, 3))
        + ((2, 0), (1, 1), (1, 3), (0, 1), (0, 3), (3, 0), (1, 0), (0, 0))
    ),
}
EXCHANGES = 4
DEPTH = 16


def unit_roots(index, modulus):
    angles = -2.0 * math.pi * (index % modulus) / modulus
    return np.cos(angles), np.sin(angles)


def three_pass(matrix, axis, tall=False):
    high = matrix.astype(ml_dtypes.bfloat16)
    low = (matrix - high.astype(np.float64)).astype(ml_dtypes.bfloat16)
    return np.concatenate([high, low] if axis == 0 and tall else [high, high, low], axis)


def tables():
    idx = np.arange(128, dtype=np.int64)
    re, im = unit_roots(idx[:, None] * idx[None, :], 128)
    left = lambda r, i: np.block([[r, -i], [i, r]])
    right = lambda r, i: np.block([[r, i], [-i, r]])
    offsets = np.arange(BLOCKS * LANES, dtype=np.int64).reshape(BLOCKS, 1, LANES)
    grid = offsets * idx[None, :, None]
    kb = np.arange(BLOCKS, dtype=np.int64)
    small = kb[:, None] * idx[None, :]
    f32 = lambda pair, axis: np.stack(pair, axis).astype(np.float32)
    return {
        "roots": f32((re, im), 0),
        "shift": f32(unit_roots(idx[:, None] * idx[None, :], 16384), 0),
        "outer": f32(unit_roots(grid, TOTAL), 1),
        "inner": f32(unit_roots(grid, SEG), 1),
        "small": f32(unit_roots(small, BLOCKS * LANES), 1),
        "left_fwd": three_pass(left(re, im), 0, True),
        "left_inv": three_pass(left(re, -im) / SEG, 0, True),
        "right_fwd": three_pass(right(re, im), 0),
        "right_inv": three_pass(right(re, -im), 0),
    }


TABLES = tables()
NAMES = tuple(TABLES)


def split(value):
    high = value.astype(BF16)
    low = (value - high.astype(F32)).astype(BF16)
    return high, low


def left_product(matrix, real, imag):
    high, low = split(jnp.concatenate([real, imag], 0))
    both = jnp.dot(matrix[:512], high, preferred_element_type=F32)
    out = both[:256] + (both[256:] + jnp.dot(matrix[:256], low, preferred_element_type=F32))
    return out[:128], out[128:]


def right_product(value, matrix):
    high, low = split(value)
    return jnp.dot(jnp.concatenate([high, low, high], 1), matrix, preferred_element_type=F32)


def times(real, imag, cos, sin):
    return real * cos - imag * sin, real * sin + imag * cos


def times_conj(real, imag, cos, sin):
    return real * cos + imag * sin, imag * cos - real * sin


def add(a, b):
    return a[0] + b[0], a[1] + b[1]


def sub(a, b):
    return a[0] - b[0], a[1] - b[1]


def quarter(a, sign):
    return (-a[1], a[0]) if sign > 0 else (a[1], -a[0])


def dft4(z, sign):
    e0, e1 = add(z[0], z[2]), sub(z[0], z[2])
    o0, o1 = add(z[1], z[3]), quarter(sub(z[1], z[3]), sign)
    return [add(e0, o0), add(e1, o1), sub(e0, o0), sub(e1, o1)]


def dft8(z, sign):
    even, odd = dft4(z[0::2], sign), dft4(z[1::2], sign)
    root = math.sqrt(0.5)
    q1 = quarter(odd[1], sign)
    q3 = quarter(odd[3], sign)
    odd = [
        odd[0],
        ((odd[1][0] + q1[0]) * root, (odd[1][1] + q1[1]) * root),
        quarter(odd[2], sign),
        ((q3[0] - odd[3][0]) * root, (q3[1] - odd[3][1]) * root),
    ]
    return [add(even[k], odd[k]) for k in range(4)] + [sub(even[k], odd[k]) for k in range(4)]


def sin_cos(angle):
    half = angle * 0.5
    sq = half * half
    sine = 0.0
    for power in (13, 11, 9, 7, 5, 3, 1):
        sine = sine * sq + (-1.0) ** (power // 2) / math.factorial(power)
    cosine = 0.0
    for power in (12, 10, 8, 6, 4, 2, 0):
        cosine = cosine * sq + (-1.0) ** (power // 2) / math.factorial(power)
    sine = sine * half
    return 2.0 * sine * cosine, 1.0 - 2.0 * sine * sine


def where_is(coord):
    every = slice(None)
    y = coord.get("y")
    return (
        every if y is None else y % 2,
        coord.get("x", every),
        coord.get("z", every),
        every if y is None else y // 2,
        coord.get("c", every),
    )


def device_at(coord):
    y = coord["y"]
    return ((y % 2) * 4 + coord["x"], coord["z"] * 4 + (y // 2) * 2 + coord["c"])


def slot(exchange, stage):
    return exchange * 3 + stage - 1


SLOTS = 3 * EXCHANGES - 2


def kernel(x_ref, chirp_ref, *refs):
    count = len(NAMES)
    table_refs, out_ref, refs = refs[:count], refs[count], refs[count + 1 :]
    held, refs = dict(zip(NAMES, refs[:count])), refs[count:]
    (bufs, chirp_in, response, work, dev_fwd, dev_inv, send_sem, recv_sem, load_sem) = refs

    row, col = lax.axis_index("row"), lax.axis_index("col")
    me = row * 16 + col
    here = {"x": row % 4, "y": row // 4 + 2 * (col // 2 % 2), "z": col // 4, "c": col % 2}

    loads = {}
    for i, (name, src) in enumerate(zip(NAMES + ("chirp",), table_refs + (chirp_ref,))):
        dst = chirp_in if name == "chirp" else held[name]
        loads[name] = pltpu.make_async_copy(src, dst, load_sem.at[i])

    def peers(axes, mirror=False):
        for steps in STEPS[axes]:
            if mirror:
                steps = tuple(-step % SIZES[axis] for axis, step in zip(axes, steps))
            there = dict(here)
            for axis, step in zip(axes, steps):
                there[axis] = (here[axis] + step) % SIZES[axis]
            yield any(steps), there

    barrier = pltpu.get_barrier_semaphore()
    greeted = [there for axes in ORDERS[0] for remote, there in peers(axes) if remote]
    for there in greeted:
        pl.semaphore_signal(barrier, inc=1, device_id=device_at(there), device_id_type=MESH)
    for name in ("roots", "shift", "chirp", "outer", "left_fwd", "inner", "small", "right_fwd", "right_inv", "left_inv"):
        loads[name].start()
    pl.semaphore_wait(barrier, len(greeted))

    def stage_ref(stream, exchange, stage):
        if exchange == 0 and stage == 0:
            return x_ref.at[stream // 2, stream % 2]
        if exchange == EXCHANGES - 1 and stage == 2:
            return out_ref.at[stream // 2, stream % 2]
        return bufs.at[stream, slot(exchange, stage)]

    def sub_ref(stream, exchange, stage, where):
        if exchange == 0 and stage == 0:
            return x_ref.at[(stream // 2,) + where + (stream % 2,)]
        if exchange == EXCHANGES - 1 and stage == 2:
            return out_ref.at[(stream // 2,) + where + (stream % 2,)]
        return bufs.at[(stream, slot(exchange, stage)) + where]

    def sem_index(exchange, phase):
        return exchange * 2 + phase

    def send(stream, exchange, phase):
        axes = ORDERS[stream][phase]
        k = sem_index(exchange, phase)
        mine = where_is({a: here[a] for a in axes})
        for remote, there in peers(axes, stream >= 2):
            src = sub_ref(stream, exchange, phase, where_is({a: there[a] for a in axes}))
            dst = sub_ref(stream, exchange, phase + 1, mine)
            if remote:
                pltpu.make_async_remote_copy(
                    src_ref=src,
                    dst_ref=dst,
                    send_sem=send_sem.at[stream, k],
                    recv_sem=recv_sem.at[stream, k],
                    device_id=device_at(there),
                    device_id_type=MESH,
                ).start()
            else:
                pltpu.make_async_copy(src, dst, recv_sem.at[stream, k]).start()

    def arrive(stream, exchange, phase):
        whole = sub_ref(stream, exchange, phase + 1, (slice(None),) * 5)
        pltpu.make_async_copy(whole, whole, recv_sem.at[stream, sem_index(exchange, phase)]).wait()

    def sent(stream, exchange, phase):
        share = math.prod(SIZES[a] for a in ORDERS[stream][phase])
        part = bufs.at[stream, 0].reshape(128, 8, 128).at[pl.ds(0, 128 - 128 // share)]
        pltpu.make_async_copy(part, part, send_sem.at[stream, sem_index(exchange, phase)]).wait()

    def flat(stream, exchange, stage):
        return bufs.at[stream, slot(exchange, stage)].reshape(1024, 128)

    def row_of(block, part):
        return pl.ds(block % 4 * 2 + part, 128, stride=8)

    def load_pair(refs2, block):
        out = []
        for part in range(2):
            out.append(
                jnp.concatenate([refs2[b // 4][row_of(b, part), :] for b in (block, block + 1)], 1)
            )
        return out

    def build_matrices():
        for name in ("roots", "shift"):
            loads[name].wait()
        re, im = held["roots"][0], held["roots"][1]
        sre, sim = held["shift"][0], held["shift"][1]
        on_lane = lax.broadcasted_iota(jnp.int32, (128, 128), 1) == me
        on_row = lax.broadcasted_iota(jnp.int32, (128, 128), 0) == me
        pick = lambda mask, v, axis: jnp.sum(jnp.where(mask, v, 0.0), axis=axis, keepdims=True)
        fre, fim = times(re, im, pick(on_lane, sre, 1), pick(on_lane, sim, 1))
        ire, iim = times(re, im, pick(on_row, sre, 0), pick(on_row, sim, 0))
        ire, iim = ire * (1.0 / PIECES), iim * (-1.0 / PIECES)
        for ref, r, i in ((dev_fwd, fre, fim), (dev_inv, ire, iim)):
            for half, (a, b) in enumerate(((r, -i), (i, r))):
                high, low = split(jnp.concatenate([a, b], 1))
                ref[pl.ds(half * 128, 128), :] = high
                ref[pl.ds(256 + half * 128, 128), :] = low

    def build_response():
        loads["chirp"].wait()
        for kb in range(BLOCKS):
            angle = chirp_in[pl.ds(kb, 128, stride=8), :].T
            sine, cosine = sin_cos(angle)
            response[kb, 0] = cosine
            response[kb, 1] = sine

    def first_step(stream):
        src, dst = flat(stream, 0, 2), flat(stream, 1, 0)
        outer = held["outer"]
        for block in range(stream % 2 * 4, stream % 2 * 4 + 4, 2):
            real, imag = load_pair((src, src), block)
            real, imag = left_product(dev_fwd[...], real, imag)
            for i in range(2):
                b = block + i
                lanes = slice(i * 128, i * 128 + 128)
                r, m = times(real[:, lanes], imag[:, lanes], outer[b, 0], outer[b, 1])
                dst[row_of(b, 0), :] = r
                dst[row_of(b, 1), :] = m

    def middle_open(stream):
        src = flat(stream, 1, 2)
        inner = held["inner"]
        for block in range(stream % 2 * 4, stream % 2 * 4 + 4, 2):
            real, imag = load_pair((src, src), block)
            real, imag = left_product(held["left_fwd"][...], real, imag)
            for i in range(2):
                b = block + i
                lanes = slice(i * 128, i * 128 + 128)
                r, m = times(real[:, lanes], imag[:, lanes], inner[b, 0], inner[b, 1])
                work[b, 0] = r
                work[b, 1] = m

    def middle_core():
        inner, small = held["inner"], held["small"]

        def part(step, _):
            rows = pl.ds(pl.multiple_of(step * DEPTH, DEPTH), DEPTH)
            z = dft8([(work[b, 0, rows, :], work[b, 1, rows, :]) for b in range(BLOCKS)], -1)
            for k in range(1, BLOCKS):
                z[k] = times(z[k][0], z[k][1], small[k, 0:1, :], small[k, 1:2, :])
            value = jnp.concatenate([jnp.concatenate(pair, 1) for pair in z], 0)
            value = right_product(value, held["right_fwd"][...])
            z = []
            for k in range(BLOCKS):
                at = slice(k * DEPTH, k * DEPTH + DEPTH)
                z.append(times(value[at, :128], value[at, 128:], response[k, 0, rows, :], response[k, 1, rows, :]))
            value = jnp.concatenate([jnp.concatenate(pair, 1) for pair in z], 0)
            value = right_product(value, held["right_inv"][...])
            z = []
            for k in range(BLOCKS):
                at = slice(k * DEPTH, k * DEPTH + DEPTH)
                r, m = value[at, :128], value[at, 128:]
                z.append(times_conj(r, m, small[k, 0:1, :], small[k, 1:2, :]) if k else (r, m))
            z = dft8(z, 1)
            for b in range(BLOCKS):
                r, m = times_conj(z[b][0], z[b][1], inner[b, 0, rows, :], inner[b, 1, rows, :])
                work[b, 0, rows, :] = r
                work[b, 1, rows, :] = m
            return 0

        lax.fori_loop(0, 128 // DEPTH, part, 0, unroll=True)

    def middle_close(stream):
        dst = flat(stream, 2, 0)
        for block in range(stream % 2 * 4, stream % 2 * 4 + 4, 2):
            real = jnp.concatenate([work[block, 0], work[block + 1, 0]], 1)
            imag = jnp.concatenate([work[block, 1], work[block + 1, 1]], 1)
            real, imag = left_product(held["left_inv"][...], real, imag)
            for i in range(2):
                b = block + i
                lanes = slice(i * 128, i * 128 + 128)
                dst[row_of(b, 0), :] = real[:, lanes]
                dst[row_of(b, 1), :] = imag[:, lanes]

    def last_step(stream):
        src, dst = flat(stream, 2, 2), flat(stream, 3, 0)
        outer = held["outer"]
        for block in range(stream % 2 * 4, stream % 2 * 4 + 4, 2):
            parts = []
            for b in (block, block + 1):
                parts.append(times_conj(src[row_of(b, 0), :], src[row_of(b, 1), :], outer[b, 0], outer[b, 1]))
            real = jnp.concatenate([p[0] for p in parts], 1)
            imag = jnp.concatenate([p[1] for p in parts], 1)
            real, imag = left_product(dev_inv[...], real, imag)
            for i in range(2):
                b = block + i
                lanes = slice(i * 128, i * 128 + 128)
                dst[row_of(b, 0), :] = real[:, lanes]
                dst[row_of(b, 1), :] = imag[:, lanes]

    def settle(step):
        if step >= 0:
            for stream in range(STREAMS):
                sent(stream, step // 2, step % 2)

    for stream in (0, 1):
        send(stream, 0, 0)
    build_matrices()
    for stream in (2, 3):
        send(stream, 0, 0)
    for exchange in range(EXCHANGES):
        for stream in range(STREAMS):
            arrive(stream, exchange, 0)
            send(stream, exchange, 1)
        if exchange == 0:
            build_response()
            for name in ("outer", "left_fwd", "inner", "small", "right_fwd", "right_inv", "left_inv"):
                loads[name].wait()
        settle(2 * exchange - 2)
        settle(2 * exchange - 1)
        for pair in range(2):
            streams = (2 * pair, 2 * pair + 1)
            for stream in streams:
                arrive(stream, exchange, 1)
                if exchange == 0:
                    first_step(stream)
                if exchange == 1:
                    middle_open(stream)
                if exchange == 2:
                    last_step(stream)
                if exchange in (0, 2):
                    send(stream, exchange + 1, 0)
            if exchange == 1:
                middle_core()
                for stream in streams:
                    middle_close(stream)
                    send(stream, exchange + 1, 0)
    settle(2 * EXCHANGES - 2)
    settle(2 * EXCHANGES - 1)


def body(voltages, chirp_phase):
    shape = (2,) + DEVICE_DIMS + (2,) + TILE
    rows = voltages.reshape(2, 2, PIECES * BLOCKS, LANES).transpose(0, 2, 1, 3).reshape(shape)
    any_space = pl.BlockSpec(memory_space=pl.ANY)
    values = [jnp.asarray(TABLES[name]) for name in NAMES]
    operands = [rows, chirp_phase.reshape(PIECES * BLOCKS, LANES)] + values
    held = [pltpu.VMEM(v.shape, v.dtype) for v in values]
    out = pl.pallas_call(
        kernel,
        out_shape=pltpu.VMEM(shape, F32),
        in_specs=[any_space] * (2 + len(values)),
        out_specs=pl.BlockSpec(memory_space=pltpu.VMEM),
        scratch_shapes=held
        + [
            pltpu.VMEM((STREAMS, SLOTS) + DEVICE_DIMS + TILE, F32),
            pltpu.VMEM((PIECES * BLOCKS, LANES), F32),
            pltpu.VMEM((BLOCKS, 2, 128, 128), F32),
            pltpu.VMEM((BLOCKS, 2, 128, 128), F32),
            pltpu.VMEM((512, 256), BF16),
            pltpu.VMEM((512, 256), BF16),
            pltpu.SemaphoreType.DMA((STREAMS, 2 * EXCHANGES)),
            pltpu.SemaphoreType.DMA((STREAMS, 2 * EXCHANGES)),
            pltpu.SemaphoreType.DMA((len(values) + 1,)),
        ],
        name="dedisperse",
        compiler_params=pltpu.CompilerParams(
            collective_id=0, has_side_effects=True, vmem_limit_bytes=48 * 1024 * 1024
        ),
        cost_estimate=pl.CostEstimate(flops=5_000_000_000, bytes_accessed=9_000_000, transcendentals=0),
    )(*[pltpu.with_memory_space_constraint(v, pltpu.HBM) for v in operands])
    return out.reshape(2, PIECES * BLOCKS, 2, LANES).transpose(0, 2, 1, 3).reshape(voltages.shape)


def solution(mesh):
    placed = (P(None, None, None, ("row", "col")), P(None, ("row", "col"), None))
    return jax.shard_map(
        body,
        mesh=mesh,
        in_specs=placed,
        out_specs=P(None, None, None, ("row", "col")),
        check_vma=False,
    )
```
